512 devices in a mesh: seq: 32 (over x, z_lo, core), chan: 16 (over z_hi, y).
Axes of the slice: x: 4, y: 4, z: 16 (z_hi: 4, z_lo: 4; z = z_hi * 4 + z_lo), core: 2. Of those that a mesh axis runs over, the one named last changes fastest.
Arguments:
- grad_out: bfloat16 [4096, 4096], P('seq', 'chan'), may hold values from -6 to 6
- query_gate: bfloat16 [4096, 4096], P('seq', 'chan'), may hold values from -6 to 6
- key_gate: bfloat16 [4096, 4096], P('seq', 'chan'), may hold values from -6 to 6
- value_input: bfloat16 [4096, 4096], P('seq', 'chan'), may hold values from -6 to 6
- filter_taps: float32 [4096, 128], P('chan'), may hold values from -2 to 2
- skip_gain: float32 [4096], P('chan'), may hold values from -1 to 1
- out_weight: bfloat16 [4096, 4096], P('chan'), may hold values from -0.09375 to 0.09375
Outputs:
- grad_query: bfloat16 [4096, 4096], P('seq', 'chan')
- grad_key: bfloat16 [4096, 4096], P('seq', 'chan')
- grad_value: bfloat16 [4096, 4096], P('seq', 'chan')
- grad_filter: float32 [4096, 128], P('chan')
- grad_skip: float32 [4096], P('chan')
- grad_weight: float32 [4096, 4096], P('chan', 'seq')
The draws below stay inside these ranges and needn't reach their ends.
All inputs are finite; a program needn't handle non-finite values.
Results may differ from the reference program's by a relative error of at most 0.0029.
Values may be sent and summed in bfloat16 or wider, within the bound.
No kernel may reach another device: no remote copies, remote signals or barrier semaphores. Data moves between devices by JAX's collectives and lax.ppermute only.
A program may use at most 128 MiB of HBM per device.

```python
import math
import jax
import jax.numpy as jnp
from jax import lax

D = 4096
TAPS = 128
TOKENS = 4096


def draw_filter_taps(key, part):
    key = jax.random.fold_in(key, 7)
    rate_key, value_key = jax.random.split(key)
    decay_rates = jnp.exp(jax.random.uniform(rate_key, (D, 1), jnp.float32, math.log(0.005), math.log(0.1)))
    raw_taps = jax.random.normal(value_key, (D, TAPS), jnp.float32)
    tap_position = jnp.arange(TAPS, dtype=jnp.float32)[None, :]
    return jnp.clip(0.15 * raw_taps * jnp.exp(-decay_rates * tap_position), -2.0, 2.0).astype(jnp.float32)


def spiked(entries, rng, source, target, shards_of, factor):
    owner, partner = [(jnp.arange(entries.shape[dim]) // (entries.shape[dim] // shards_of)).reshape([-1 if axis == dim else 1 for axis in range(entries.ndim)]) for dim in (source, target)]
    chosen = jax.random.permutation(rng, shards_of)[partner]
    strong = (owner == chosen) | (owner == (partner + shards_of // 2) % shards_of)
    return jnp.where(strong, factor * entries, entries)


def levels(own_key, extent, cuts, least, largest):
    level = 1.0
    for dim, shards_of in cuts:
        draws = jax.random.uniform(jax.random.fold_in(jax.random.fold_in(own_key, 6), dim), (shards_of,), jnp.float32, least / len(cuts), largest / len(cuts))
        level = level * jnp.repeat(jnp.exp(draws), extent[dim] // shards_of).reshape((-1,) + (1,) * (len(extent) - 1 - dim))
    return level


def bell_draw(stream_key, extent, spread, most, shards=(), held_as=jnp.bfloat16):
    loudness = levels(stream_key, extent, shards, -0.22, 0.18) if shards else 1.0
    drawn = jax.random.normal(stream_key, extent, jnp.float32) * spread * loudness
    return jnp.minimum(jnp.maximum(drawn, -most), most).astype(held_as)


def bell_draw_with(own_key, shape, spread, most, cuts, heavy, held_as=jnp.bfloat16):
    array = spread * jax.random.normal(own_key, shape, jnp.float32)
    if cuts:
        array = array * levels(own_key, shape, cuts, -0.22, 0.18)
    return jnp.clip(spiked(array, jax.random.fold_in(own_key, 3), *heavy), -most, most).astype(held_as)


def setup_inputs(seed: int = 0) -> dict:
    keys = jax.random.split(jax.random.key(seed), 8)
    return {
        "grad_out": bell_draw_with(keys[0], (TOKENS, D), 1.0, 6.0, ((0, 32), (1, 16)), (0, 1, 32, 2.75)),
        "query_gate": bell_draw(keys[1], (TOKENS, D), 1.0, 6.0, ((0, 32), (1, 16))),
        "key_gate": bell_draw(keys[2], (TOKENS, D), 1.0, 6.0, ((0, 32), (1, 16))),
        "value_input": bell_draw(keys[3], (TOKENS, D), 1.0, 6.0, ((0, 32), (1, 16))),
        "filter_taps": draw_filter_taps(jax.random.fold_in(keys[7], 71), 0),
        "skip_gain": jnp.clip(jax.random.uniform(keys[5], (D,), jnp.float32, -1.0, 1.0) * levels(keys[5], (D,), ((0, 16),), -0.4, 0.0), -1.0, 1.0),
        "out_weight": bell_draw(keys[6], (D, D), D ** -0.5, 0.09375, ((0, 16),)),
    }


def causal_sum(padded, tap_values, length):
    running = jnp.zeros((length, padded.shape[1]), jnp.float32)
    for tap_index in range(TAPS):
        offset = TAPS - 1 - tap_index
        running = running + tap_values[:, tap_index] * padded[offset:offset + length]
    return running

def ahead_sum(padded, tap_values, length):
    running = jnp.zeros((length, padded.shape[1]), jnp.float32)
    for tap_index in range(TAPS):
        running = running + tap_values[:, tap_index] * padded[tap_index:tap_index + length]
    return running

def tap_products(grad_sum, padded, length):
    columns = []
    for tap_index in range(TAPS):
        offset = TAPS - 1 - tap_index
        columns.append(lax.optimization_barrier(jnp.sum(grad_sum * padded[offset:offset + length], axis=0)))
    return jnp.stack(columns, axis=1)

def reference(grad_out, query_gate, key_gate, value_input, filter_taps, skip_gain, out_weight):
    norm_factor = 1.0 / math.sqrt(TOKENS)
    width = 256
    blocks = D // width

    def channel_block(index):
        lower = (index * width).astype(jnp.int32)
        weight_rows = lax.dynamic_slice_in_dim(out_weight, lower, width, 0)
        grad_mixed = lax.dot_general(grad_out, weight_rows, (((1,), (1,)), ((), ())), preferred_element_type=jnp.float32)
        query_part = lax.dynamic_slice_in_dim(query_gate, lower, width, 1).astype(jnp.float32)
        key_part = lax.dynamic_slice_in_dim(key_gate, lower, width, 1).astype(jnp.float32)
        value_part = lax.dynamic_slice_in_dim(value_input, lower, width, 1).astype(jnp.float32)
        tap_values = lax.dynamic_slice_in_dim(filter_taps, lower, width, 0)
        gain = lax.dynamic_slice_in_dim(skip_gain, lower, width, 0)
        mixed_in = key_part * value_part
        padded = jnp.concatenate([jnp.zeros((TAPS - 1, width), jnp.float32), mixed_in], axis=0)
        summed = causal_sum(padded, tap_values, TOKENS) + gain * mixed_in
        mixer_out = (query_part * summed).astype(jnp.bfloat16)
        grad_query = (grad_mixed * summed).astype(jnp.bfloat16)
        grad_sum = grad_mixed * query_part
        padded_grad = jnp.concatenate([grad_sum, jnp.zeros((TAPS - 1, width), jnp.float32)], axis=0)
        grad_mix = ahead_sum(padded_grad, tap_values, TOKENS) + gain * grad_sum
        grad_key = (grad_mix * value_part).astype(jnp.bfloat16)
        grad_value = (grad_mix * key_part).astype(jnp.bfloat16)
        grad_filter = tap_products(grad_sum, padded, TOKENS) * norm_factor
        grad_skip = lax.optimization_barrier(jnp.sum(grad_sum * mixed_in, axis=0)) * norm_factor
        return (mixer_out, grad_query, grad_key, grad_value, grad_filter, grad_skip)
    results = lax.map(channel_block, jnp.arange(blocks, dtype=jnp.int32))

    def tokens_major(stacked):
        return jnp.transpose(stacked, (1, 0, 2)).reshape(TOKENS, D)
    mixer_out = tokens_major(results[0])
    grad_query = tokens_major(results[1])
    grad_key = tokens_major(results[2])
    grad_value = tokens_major(results[3])
    grad_filter = results[4].reshape(D, TAPS)
    grad_skip = results[5].reshape(D)
    grad_weight = lax.dot_general(mixer_out, grad_out, (((0,), (0,)), ((), ())), preferred_element_type=jnp.float32) * norm_factor
    return (grad_query, grad_key, grad_value, grad_filter, grad_skip, grad_weight)
```

```python
import math

import jax
import jax.numpy as jnp
from jax import lax
from jax.experimental import pallas as pl
from jax.experimental.pallas import tpu as pltpu
from jax.sharding import PartitionSpec as P

TAPS = 128
LANES = 128
SUB = 8
XS, ZL, CORES = 4, 4, 2
ZH, YS = 4, 4
F32 = jnp.float32
BF16 = jnp.bfloat16


def seq_index(x, zl, core):
    return (x * ZL + zl) * CORES + core


def chan_index(zh, y):
    return zh * YS + y


ZH_GROUPS = [[chan_index(zh, y) for zh in range(ZH)] for y in range(YS)]
Y_GROUPS = [[chan_index(zh, y) for y in range(YS)] for zh in range(ZH)]
XC_GROUPS = [
    [seq_index(x, zl, core) for x in range(XS) for core in range(CORES)] for zl in range(ZL)
]
ZL_GROUPS = [
    [seq_index(x, zl, core) for zl in range(ZL)] for x in range(XS) for core in range(CORES)
]


def exchange(value, axis, groups):
    return lax.all_to_all(value, axis, 0, 0, tiled=True, axis_index_groups=groups)


def spread(value, axis, groups, size):
    return exchange(jnp.broadcast_to(value[None], (size, *value.shape)), axis, groups)


def passed_along(value, axis, by):
    size = lax.axis_size(axis)
    pairs = [(i, i + by) for i in range(size) if 0 <= i + by < size]
    return lax.ppermute(value, axis, pairs)


def causal_kernel(prev_ref, mixed_ref, taps_ref, gain_ref, query_ref, summed_ref, out_ref, pad):
    rows, width = mixed_ref.shape
    pad[:rows] = prev_ref[...]
    pad[rows:] = mixed_ref[...]
    for lane in range(0, width, LANES):
        cols = pl.ds(lane, LANES)
        tap_rows = taps_ref[cols, :].T
        total = gain_ref[:, cols] * mixed_ref[:, cols]
        for r in range(SUB):
            shifted = pad[pl.ds(SUB - r, 2 * rows - SUB), cols]
            for q in range(TAPS // SUB):
                start = rows - SUB - SUB * q
                j = SUB * q + r
                total = total + tap_rows[j : j + 1] * shifted[start : start + rows]
        summed_ref[:, cols] = total
        out_ref[:, cols] = (query_ref[:, cols].astype(F32) * total).astype(BF16)


def project_kernel(gathered_ref, weight_ref, query_ref, summed_ref, grad_query_ref, grad_sum_ref):
    width = gathered_ref.shape[-1]
    total = None
    for y in range(YS):
        for zh in range(ZH):
            block = weight_ref[:, pl.ds(chan_index(zh, y) * width, width)]
            term = lax.dot_general(
                gathered_ref[y, zh], block, (((1,), (1,)), ((), ())), preferred_element_type=F32
            )
            total = term if total is None else total + term
    grad_query_ref[...] = (total * summed_ref[...]).astype(BF16)
    grad_sum_ref[...] = total * query_ref[...].astype(F32)


def taps_kernel(norm_factor, prev_ref, mixed_ref, grad_sum_ref, out_ref, pad, rows_ref):
    rows, width = mixed_ref.shape
    pad[:rows] = prev_ref[...]
    pad[rows:] = mixed_ref[...]
    for lane in range(0, width, LANES):
        cols = pl.ds(lane, LANES)
        grad_sum = grad_sum_ref[:, cols]
        for r in range(SUB):
            shifted = pad[pl.ds(SUB - r, 2 * rows - SUB), cols]
            for q in range(TAPS // SUB):
                start = rows - SUB - SUB * q
                j = SUB * q + r
                rows_ref[j : j + 1, :] = jnp.sum(
                    grad_sum * shifted[start : start + rows], axis=0, keepdims=True
                )
        out_ref[cols, :] = rows_ref[...].T * norm_factor


def ahead_kernel(
    grad_sum_ref, incoming_ref, taps_ref, gain_ref, key_ref, value_ref, grad_key_ref, grad_value_ref, pad
):
    rows, width = grad_sum_ref.shape
    pad[:rows] = grad_sum_ref[...]
    pad[rows:] = incoming_ref[...]
    for lane in range(0, width, LANES):
        cols = pl.ds(lane, LANES)
        tap_rows = taps_ref[cols, :].T
        total = gain_ref[:, cols] * grad_sum_ref[:, cols]
        for r in range(SUB):
            shifted = pad[pl.ds(r, 2 * rows - SUB), cols]
            for q in range(TAPS // SUB):
                start = SUB * q
                j = SUB * q + r
                total = total + tap_rows[j : j + 1] * shifted[start : start + rows]
        grad_key_ref[:, cols] = (total * value_ref[:, cols].astype(F32)).astype(BF16)
        grad_value_ref[:, cols] = (total * key_ref[:, cols].astype(F32)).astype(BF16)


def weight_kernel(mixer_ref, pieces_ref, out_ref):
    for part in range(ZL):
        total = None
        for source in range(XS * CORES):
            term = lax.dot_general(
                mixer_ref[source],
                pieces_ref[source, part],
                (((0,), (0,)), ((), ())),
                preferred_element_type=F32,
            )
            total = term if total is None else total + term
        out_ref[part] = total.astype(BF16)


def call(kernel, name, shapes, scratch, flops, moved):
    return pl.pallas_call(
        kernel,
        out_shape=shapes,
        scratch_shapes=scratch,
        name=name,
        compiler_params=pltpu.CompilerParams(vmem_limit_bytes=32 * 1024 * 1024),
        cost_estimate=pl.CostEstimate(flops=flops, bytes_accessed=moved, transcendentals=0),
    )


def body(grad_out, query_gate, key_gate, value_input, filter_taps, skip_gain, out_weight):
    rows, width = query_gate.shape
    norm_factor = 1.0 / math.sqrt(rows * lax.axis_size("seq"))
    gain = skip_gain.reshape(1, width)
    block_f32 = jax.ShapeDtypeStruct((rows, width), F32)
    block_bf16 = jax.ShapeDtypeStruct((rows, width), BF16)
    padded = pltpu.VMEM((2 * rows, width), F32)
    size = rows * width

    mixed_in = key_gate.astype(F32) * value_input.astype(F32)
    previous = passed_along(mixed_in, "seq", 1)
    over_zh = spread(grad_out, "chan", ZH_GROUPS, ZH)
    gathered = spread(over_zh, "chan", Y_GROUPS, YS)
    gathered = gathered.reshape(YS, ZH, rows, width)

    summed, mixer_out = call(
        causal_kernel, "causal", (block_f32, block_bf16), [padded], 2 * size * TAPS, 20 * size
    )(previous, mixed_in, filter_taps, gain, query_gate)
    mixers = spread(mixer_out, "seq", XC_GROUPS, XS * CORES)

    grad_query, grad_sum = call(
        project_kernel, "project", (block_bf16, block_f32), [], 2 * size * 4096, 3 * 1024 * 1024
    )(gathered, out_weight, query_gate, summed)
    incoming = passed_along(grad_sum, "seq", -1)

    pieces = gathered.reshape(YS, ZH, rows, CORES, LANES).transpose(1, 3, 0, 2, 4)
    pieces = exchange(pieces.reshape(ZH * CORES, YS, rows, LANES), "seq", XC_GROUPS)

    filter_term = call(
        lambda *refs: taps_kernel(norm_factor, *refs),
        "taps",
        jax.ShapeDtypeStruct((width, TAPS), F32),
        [padded, pltpu.VMEM((TAPS, LANES), F32)],
        2 * size * TAPS,
        16 * size,
    )(previous, mixed_in, grad_sum)
    seq_size = lax.axis_size("seq")
    share = exchange(filter_term.reshape(seq_size, width // seq_size, TAPS), "seq", None)
    grad_filter = spread(jnp.sum(share, axis=0), "seq", None, seq_size).reshape(width, TAPS)
    grad_skip = grad_filter[:, 0]

    grad_key, grad_value = call(
        ahead_kernel, "ahead", (block_bf16, block_bf16), [padded], 2 * size * TAPS, 20 * size
    )(grad_sum, incoming, filter_taps, gain, key_gate, value_input)

    partial = call(
        weight_kernel,
        "weight",
        jax.ShapeDtypeStruct((ZL, width, LANES), BF16),
        [],
        2 * XS * CORES * rows * width * ZL * LANES,
        2 * 1024 * 1024,
    )(mixers, pieces)
    terms = exchange(partial, "seq", ZL_GROUPS)
    grad_weight = jnp.sum(terms.astype(F32), axis=0) * norm_factor
    return (grad_query, grad_key, grad_value, grad_filter, grad_skip, grad_weight)


def solution(mesh):
    return jax.shard_map(
        body,
        mesh=mesh,
        in_specs=(
            P("seq", "chan"),
            P("seq", "chan"),
            P("seq", "chan"),
            P("seq", "chan"),
            P("chan", None),
            P("chan"),
            P("chan", None),
        ),
        out_specs=(
            P("seq", "chan"),
            P("seq", "chan"),
            P("seq", "chan"),
            P("chan", None),
            P("chan"),
            P("chan", "seq"),
        ),
        check_vma=False,
    )
```

```python
import math

import jax
import jax.numpy as jnp
from jax import lax
from jax.experimental import pallas as pl
from jax.experimental.pallas import tpu as pltpu
from jax.sharding import PartitionSpec as P

TAPS = 128
LANES = 128
SUB = 8
XS, ZL, CORES = 4, 4, 2
ZH, YS = 4, 4
F32 = jnp.float32
BF16 = jnp.bfloat16


def seq_index(x, zl, core):
    return (x * ZL + zl) * CORES + core


def chan_index(zh, y):
    return zh * YS + y


ZH_GROUPS = [[chan_index(zh, y) for zh in range(ZH)] for y in range(YS)]
Y_GROUPS = [[chan_index(zh, y) for y in range(YS)] for zh in range(ZH)]
XC_GROUPS = [
    [seq_index(x, zl, core) for x in range(XS) for core in range(CORES)] for zl in range(ZL)
]
ZL_GROUPS = [
    [seq_index(x, zl, core) for zl in range(ZL)] for x in range(XS) for core in range(CORES)
]
X_GROUPS = [
    [seq_index(x, zl, core) for x in range(XS)] for zl in range(ZL) for core in range(CORES)
]


def exchange(value, axis, groups):
    return lax.all_to_all(value, axis, 0, 0, tiled=True, axis_index_groups=groups)


def spread(value, axis, groups, size):
    return exchange(jnp.broadcast_to(value[None], (size, *value.shape)), axis, groups)


def collect(value, groups):
    return lax.all_gather(value, "seq", axis=0, axis_index_groups=groups)


def other_core(value):
    size = lax.axis_size("seq")
    return lax.ppermute(value, "seq", [(i, i ^ 1) for i in range(size)])


def passed_along(value, axis, by):
    size = lax.axis_size(axis)
    pairs = [(i, i + by) for i in range(size) if 0 <= i + by < size]
    return lax.ppermute(value, axis, pairs)


def fetch(sources, held, sem, first=0):
    copies = [
        pltpu.make_async_copy(source, target, sem.at[first + at])
        for at, (source, target) in enumerate(zip(sources, held))
    ]
    for copy in copies:
        copy.start()
    return copies


def finish(copies):
    for copy in copies:
        copy.wait()


def causal_kernel(
    prev_ref,
    mixed_ref,
    taps_ref,
    gain_ref,
    query_ref,
    summed_ref,
    out_ref,
    pad,
    query,
    summed,
    out,
    sem,
):
    copies = fetch((query_ref,), (query,), sem)
    rows, width = mixed_ref.shape
    pad[:rows] = prev_ref[...]
    pad[rows:] = mixed_ref[...]
    for lane in range(0, width, LANES):
        cols = pl.ds(lane, LANES)
        tap_rows = taps_ref[cols, :].T
        total = gain_ref[:, cols] * mixed_ref[:, cols]
        for r in range(SUB):
            shifted = pad[pl.ds(SUB - r, 2 * rows - SUB), cols]
            for q in range(TAPS // SUB):
                start = rows - SUB - SUB * q
                j = SUB * q + r
                total = total + tap_rows[j : j + 1] * shifted[start : start + rows]
        summed[:, cols] = total
        if lane == 0:
            finish(copies)
        out[lane // LANES] = (query[:, cols].astype(F32) * total).T.astype(BF16)
    finish(fetch((summed, out), (summed_ref, out_ref), sem, 1))


def main_kernel(
    norm_factor,
    gathered_ref,
    mixer_ref,
    weight_ref,
    query_ref,
    summed_ref,
    prev_ref,
    mixed_ref,
    grad_query_ref,
    grad_sum_ref,
    filter_ref,
    packed_ref,
    held,
    mixers,
    query,
    summed,
    pad,
    tap_rows,
    weight_sem,
    pack_sem,
    sem,
):
    rows, width = mixed_ref.shape
    blocks = fetch((mixer_ref, query_ref, summed_ref), (mixers, query, summed), sem)
    loads = []
    for zh in range(ZH):
        cols = pl.ds(zh * YS * width, YS * width)
        loads.append(pltpu.make_async_copy(weight_ref.at[:, cols], held.at[zh], weight_sem.at[zh]))
        loads[-1].start()
    packs = []
    for zh in range(ZH):
        for core in range(CORES):
            target = zh * CORES + core
            for y in range(YS):
                source = gathered_ref.at[y, zh, :, pl.ds(core * LANES, LANES)]
                packs.append(
                    pltpu.make_async_copy(source, packed_ref.at[target, y], pack_sem.at[target, y])
                )
            place = packed_ref.at[target, pl.ds(YS, mixers.shape[0])]
            packs.append(pltpu.make_async_copy(mixers, place, pack_sem.at[target, YS]))
    finish(blocks)
    for copy in packs:
        copy.start()

    total = None
    for zh in range(ZH):
        loads[zh].wait()
        for y in range(YS):
            term = lax.dot_general(
                gathered_ref[y, zh],
                held[zh, :, pl.ds(y * width, width)],
                (((1,), (1,)), ((), ())),
                preferred_element_type=F32,
            )
            total = term if total is None else total + term
    grad_query_ref[...] = (total * summed[...]).astype(BF16)
    grad_sum_ref[...] = total * query[...].astype(F32)

    pad[:rows] = prev_ref[...]
    pad[rows:] = mixed_ref[...]
    for lane in range(0, width, LANES):
        cols = pl.ds(lane, LANES)
        grad_sum = grad_sum_ref[:, cols]
        for r in range(SUB):
            shifted = pad[pl.ds(SUB - r, 2 * rows - SUB), cols]
            for q in range(TAPS // SUB):
                start = rows - SUB - SUB * q
                j = SUB * q + r
                tap_rows[j : j + 1, :] = jnp.sum(
                    grad_sum * shifted[start : start + rows], axis=0, keepdims=True
                )
        filter_ref[cols, :] = tap_rows[...].T * norm_factor
    finish(packs)


def ahead_kernel(
    grad_sum_ref,
    incoming_ref,
    taps_ref,
    gain_ref,
    key_ref,
    value_ref,
    grad_key_ref,
    grad_value_ref,
    pad,
    key,
    value,
    sem,
):
    copies = fetch((key_ref, value_ref), (key, value), sem)
    rows, width = grad_sum_ref.shape
    pad[:rows] = grad_sum_ref[...]
    pad[rows:] = incoming_ref[...]
    for lane in range(0, width, LANES):
        cols = pl.ds(lane, LANES)
        tap_rows = taps_ref[cols, :].T
        total = gain_ref[:, cols] * grad_sum_ref[:, cols]
        for r in range(SUB):
            shifted = pad[pl.ds(r, 2 * rows - SUB), cols]
            for q in range(TAPS // SUB):
                start = SUB * q
                j = SUB * q + r
                total = total + tap_rows[j : j + 1] * shifted[start : start + rows]
        if lane == 0:
            finish(copies)
        grad_key_ref[:, cols] = (total * value[:, cols].astype(F32)).astype(BF16)
        grad_value_ref[:, cols] = (total * key[:, cols].astype(F32)).astype(BF16)


def weight_kernel(pieces_ref, out_ref):
    def side_by_side(blocks):
        return jnp.concatenate(blocks, axis=1)

    halves = pieces_ref.shape[1] - ZL
    for pair in range(0, ZL, 2):
        total = None
        for x in range(XS):
            sources = range(CORES * x, CORES * (x + 1))
            mixers = jnp.concatenate(
                [side_by_side([pieces_ref[at, ZL + half] for at in sources]) for half in range(halves)],
                axis=0,
            )
            tokens = jnp.concatenate(
                [side_by_side([pieces_ref[at, pair + k] for k in range(2)]) for at in sources], axis=0
            )
            term = jnp.dot(mixers, tokens, preferred_element_type=F32)
            total = term if total is None else total + term
        for k in range(2):
            out_ref[pair + k] = total[:, k * LANES : (k + 1) * LANES].astype(BF16)


def call(kernel, name, shapes, scratch, flops, moved, vmem=32, **specs):
    return pl.pallas_call(
        kernel,
        out_shape=shapes,
        scratch_shapes=scratch,
        name=name,
        compiler_params=pltpu.CompilerParams(vmem_limit_bytes=vmem * 1024 * 1024),
        cost_estimate=pl.CostEstimate(flops=flops, bytes_accessed=moved, transcendentals=0),
        **specs,
    )


def body(grad_out, query_gate, key_gate, value_input, filter_taps, skip_gain, out_weight):
    rows, width = query_gate.shape
    norm_factor = 1.0 / math.sqrt(rows * lax.axis_size("seq"))
    gain = skip_gain.reshape(1, width)
    block_f32 = jax.ShapeDtypeStruct((rows, width), F32)
    block_bf16 = jax.ShapeDtypeStruct((rows, width), BF16)
    padded = pltpu.VMEM((2 * rows, width), F32)
    held_f32, held_bf16 = pltpu.VMEM((rows, width), F32), pltpu.VMEM((rows, width), BF16)
    in_vmem = pl.BlockSpec(memory_space=pltpu.VMEM)
    in_hbm = pl.BlockSpec(memory_space=pltpu.HBM)
    stay = lambda value: pltpu.with_memory_space_constraint(value, pltpu.HBM)
    query, key, value = stay(query_gate), stay(key_gate), stay(value_input)
    weight = stay(out_weight)
    halves = width // LANES
    held_mixers = pltpu.VMEM((halves, LANES, rows), BF16)
    size = rows * width

    mixed_in = key_gate.astype(F32) * value_input.astype(F32)
    previous = passed_along(mixed_in, "seq", 1)
    over_zh = lax.all_gather(grad_out, "chan", axis=0, axis_index_groups=ZH_GROUPS)
    gathered = spread(over_zh, "chan", Y_GROUPS, YS)
    gathered = gathered.reshape(YS, ZH, rows, width)
    summed, mixer_out = call(
        causal_kernel,
        "causal",
        (pltpu.HBM((rows, width), F32), pltpu.HBM((halves, LANES, rows), BF16)),
        [
            padded,
            held_bf16,
            held_f32,
            held_mixers,
            pltpu.SemaphoreType.DMA((3,)),
        ],
        2 * size * TAPS,
        20 * size,
        in_specs=[in_vmem, in_vmem, in_vmem, in_vmem, in_hbm],
        out_specs=[in_hbm, in_hbm],
    )(previous, mixed_in, filter_taps, gain, query)

    targets, blocks = ZH * CORES, YS + halves
    grad_query, grad_sum, filter_term, packed = call(
        lambda *refs: main_kernel(norm_factor, *refs),
        "main",
        (
            block_bf16,
            block_f32,
            jax.ShapeDtypeStruct((width, TAPS), F32),
            pltpu.HBM((targets, blocks, rows, LANES), BF16),
        ),
        [
            pltpu.VMEM((ZH, width, YS * width), BF16),
            held_mixers,
            held_bf16,
            held_f32,
            padded,
            pltpu.VMEM((TAPS, LANES), F32),
            pltpu.SemaphoreType.DMA((ZH,)),
            pltpu.SemaphoreType.DMA((targets, YS + 1)),
            pltpu.SemaphoreType.DMA((3,)),
        ],
        2 * size * (4096 + TAPS),
        8 * 1024 * 1024,
        in_specs=[in_vmem, in_hbm, in_hbm, in_hbm, in_hbm, in_vmem, in_vmem],
        out_specs=[in_vmem, in_vmem, in_vmem, in_hbm],
    )(gathered, stay(mixer_out), weight, query, stay(summed), previous, mixed_in)
    pieces = exchange(packed, "seq", XC_GROUPS)
    incoming = passed_along(grad_sum, "seq", -1)
    from_core = other_core(filter_term)
    grad_key, grad_value = call(
        ahead_kernel,
        "ahead",
        (block_bf16, block_bf16),
        [
            padded,
            held_bf16,
            held_bf16,
            pltpu.SemaphoreType.DMA((2,)),
        ],
        2 * size * TAPS,
        20 * size,
        in_specs=[in_vmem, in_vmem, in_vmem, in_vmem, in_hbm, in_hbm],
    )(grad_sum, incoming, filter_taps, gain, key, value)
    from_core, grad_key, grad_value = lax.optimization_barrier((from_core, grad_key, grad_value))
    filter_term = (filter_term + from_core).astype(BF16)
    filter_term = jnp.sum(collect(filter_term, ZL_GROUPS).astype(F32), axis=0)

    pieces, filter_term = lax.optimization_barrier((pieces, filter_term))
    partial = call(
        weight_kernel,
        "weight",
        jax.ShapeDtypeStruct((ZL, width, LANES), BF16),
        [],
        2 * XS * CORES * rows * width * ZL * LANES,
        2 * 1024 * 1024,
    )(pieces)
    partial, filter_term = lax.optimization_barrier((partial, filter_term))
    terms = exchange(partial, "seq", ZL_GROUPS)
    grad_filter = jnp.sum(collect(filter_term, X_GROUPS), axis=0)
    grad_skip = grad_filter[:, 0]
    grad_weight = jnp.sum(terms.astype(F32), axis=0) * norm_factor
    return (grad_query, grad_key, grad_value, grad_filter, grad_skip, grad_weight)


def solution(mesh):
    return jax.shard_map(
        body,
        mesh=mesh,
        in_specs=(
            P("seq", "chan"),
            P("seq", "chan"),
            P("seq", "chan"),
            P("seq", "chan"),
            P("chan", None),
            P("chan"),
            P("chan", None),
        ),
        out_specs=(
            P("seq", "chan"),
            P("seq", "chan"),
            P("seq", "chan"),
            P("chan", None),
            P("chan"),
            P("chan", "seq"),
        ),
        check_vma=False,
    )
```

```python
import math

import jax
import jax.numpy as jnp
from jax import lax
from jax.experimental import pallas as pl
from jax.experimental.pallas import tpu as pltpu
from jax.sharding import PartitionSpec as P

TAPS = 128
LANES = 128
SUB = 8
XS, ZL, CORES = 4, 4, 2
ZH, YS = 4, 4
F32 = jnp.float32
BF16 = jnp.bfloat16


def seq_index(x, zl, core):
    return (x * ZL + zl) * CORES + core


def chan_index(zh, y):
    return zh * YS + y


ZH_GROUPS = [[chan_index(zh, y) for zh in range(ZH)] for y in range(YS)]
Y_GROUPS = [[chan_index(zh, y) for y in range(YS)] for zh in range(ZH)]
XC_GROUPS = [
    [seq_index(x, zl, core) for x in range(XS) for core in range(CORES)] for zl in range(ZL)
]
ZL_GROUPS = [
    [seq_index(x, zl, core) for zl in range(ZL)] for x in range(XS) for core in range(CORES)
]
X_GROUPS = [
    [seq_index(x, zl, core) for x in range(XS)] for zl in range(ZL) for core in range(CORES)
]
CORE_GROUPS = [
    [seq_index(x, zl, core) for core in range(CORES)] for x in range(XS) for zl in range(ZL)
]


def exchange(value, axis, groups):
    return lax.all_to_all(value, axis, 0, 0, tiled=True, axis_index_groups=groups)


def spread(value, axis, groups, size):
    return exchange(jnp.broadcast_to(value[None], (size, *value.shape)), axis, groups)


def collect(value, groups):
    return lax.all_gather(value, "seq", axis=0, axis_index_groups=groups)


def other_z(value, flip):
    pairs = [
        (seq_index(x, zl, core), seq_index(x, zl ^ flip, core))
        for x in range(XS)
        for zl in range(ZL)
        for core in range(CORES)
    ]
    return lax.ppermute(value, "seq", pairs)


def passed_along(value, axis, by):
    size = lax.axis_size(axis)
    pairs = [(i, i + by) for i in range(size) if 0 <= i + by < size]
    return lax.ppermute(value, axis, pairs)


def fetch(sources, held, sem, first=0):
    copies = [
        pltpu.make_async_copy(source, target, sem.at[first + at])
        for at, (source, target) in enumerate(zip(sources, held))
    ]
    for copy in copies:
        copy.start()
    return copies


def finish(copies):
    for copy in copies:
        copy.wait()


def weighted(shifted, tap_rows, starts, rows):
    part = None
    for tap, start in starts:
        term = tap_rows[tap : tap + 1, :] * shifted[start : start + rows]
        part = term if part is None else part + term
    return part


def causal_kernel(
    prev_ref,
    mixed_ref,
    taps_ref,
    gain_ref,
    query_ref,
    summed_ref,
    packed_ref,
    pad,
    tap_rows,
    query,
    summed,
    mixers,
    sem,
):
    copies = fetch((query_ref,), (query,), sem)
    rows, width = mixed_ref.shape
    pad[:rows] = prev_ref[...]
    pad[rows:] = mixed_ref[...]
    for lane in range(0, width, LANES):
        cols = pl.ds(lane, LANES)
        tap_rows[...] = taps_ref[cols, :].T
        total = gain_ref[:, cols] * mixed_ref[:, cols]
        for r in range(SUB):
            shifted = pad[pl.ds(SUB - r, 2 * rows - SUB), cols]
            starts = [(SUB * q + r, rows - SUB - SUB * q) for q in range(TAPS // SUB)]
            total = total + weighted(shifted, tap_rows, starts, rows)
        summed[:, cols] = total
        if lane == 0:
            finish(copies)
        mixers[lane // LANES] = (query[:, cols].astype(F32) * total).T.astype(BF16)
    targets, halves = packed_ref.shape[0], mixers.shape[0]
    places = [packed_ref.at[target, pl.ds(YS, halves)] for target in range(targets)]
    finish(fetch([summed] + [mixers] * targets, [summed_ref] + places, sem, 1))


def pack_kernel(gathered_ref, begun_ref, packed_ref, sem):
    del begun_ref
    packs = []
    for zh in range(ZH):
        for core in range(CORES):
            target = zh * CORES + core
            for y in range(YS):
                source = gathered_ref.at[y, zh, :, pl.ds(core * LANES, LANES)]
                packs.append(
                    pltpu.make_async_copy(source, packed_ref.at[target, y], sem.at[target, y])
                )
                packs[-1].start()
    finish(packs)


def main_kernel(
    norm_factor,
    gathered_ref,
    weight_ref,
    query_ref,
    summed_ref,
    prev_ref,
    mixed_ref,
    grad_query_ref,
    grad_sum_ref,
    filter_ref,
    held,
    query,
    summed,
    pad,
    tap_rows,
    weight_sem,
    sem,
):
    rows, width = mixed_ref.shape
    loads = []
    for zh in range(ZH):
        cols = pl.ds(zh * YS * width, YS * width)
        loads.append(pltpu.make_async_copy(weight_ref.at[:, cols], held.at[zh], weight_sem.at[zh]))
        loads[-1].start()
    blocks = fetch((query_ref, summed_ref), (query, summed), sem)
    pad[:rows] = prev_ref[...]
    pad[rows:] = mixed_ref[...]

    total = None
    for zh in range(ZH):
        loads[zh].wait()
        for y in range(YS):
            term = lax.dot_general(
                gathered_ref[y, zh],
                held[zh, :, pl.ds(y * width, width)],
                (((1,), (1,)), ((), ())),
                preferred_element_type=F32,
            )
            total = term if total is None else total + term
    finish(blocks)
    grad_query_ref[...] = (total * summed[...]).astype(BF16)
    grad_sum_ref[...] = total * query[...].astype(F32)

    for lane in range(0, width, LANES):
        cols = pl.ds(lane, LANES)
        grad_sum = grad_sum_ref[:, cols]
        for r in range(SUB):
            shifted = pad[pl.ds(SUB - r, 2 * rows - SUB), cols]
            for q in range(TAPS // SUB):
                start = rows - SUB - SUB * q
                j = SUB * q + r
                tap_rows[j : j + 1, :] = jnp.sum(
                    grad_sum * shifted[start : start + rows], axis=0, keepdims=True
                )
        filter_ref[cols, :] = tap_rows[...].T * norm_factor


def ahead_kernel(
    grad_sum_ref,
    incoming_ref,
    taps_ref,
    gain_ref,
    key_ref,
    value_ref,
    grad_key_ref,
    grad_value_ref,
    pad,
    tap_rows,
    key,
    value,
    sem,
):
    copies = fetch((key_ref, value_ref), (key, value), sem)
    rows, width = grad_sum_ref.shape
    pad[:rows] = grad_sum_ref[...]
    pad[rows:] = incoming_ref[...]
    for lane in range(0, width, LANES):
        cols = pl.ds(lane, LANES)
        tap_rows[...] = taps_ref[cols, :].T
        total = gain_ref[:, cols] * grad_sum_ref[:, cols]
        for r in range(SUB):
            shifted = pad[pl.ds(r, 2 * rows - SUB), cols]
            starts = [(SUB * q + r, SUB * q) for q in range(TAPS // SUB)]
            total = total + weighted(shifted, tap_rows, starts, rows)
        if lane == 0:
            finish(copies)
        grad_key_ref[:, cols] = (total * value[:, cols].astype(F32)).astype(BF16)
        grad_value_ref[:, cols] = (total * key[:, cols].astype(F32)).astype(BF16)


def weight_kernel(pieces_ref, out_ref):
    def side_by_side(blocks):
        return jnp.concatenate(blocks, axis=1)

    halves = pieces_ref.shape[1] - ZL
    for pair in range(0, ZL, 2):
        total = None
        for x in range(XS):
            sources = range(CORES * x, CORES * (x + 1))
            mixers = jnp.concatenate(
                [side_by_side([pieces_ref[at, ZL + half] for at in sources]) for half in range(halves)],
                axis=0,
            )
            tokens = jnp.concatenate(
                [side_by_side([pieces_ref[at, pair + k] for k in range(2)]) for at in sources], axis=0
            )
            term = jnp.dot(mixers, tokens, preferred_element_type=F32)
            total = term if total is None else total + term
        for k in range(2):
            out_ref[pair + k] = total[:, k * LANES : (k + 1) * LANES].astype(BF16)


def finish_kernel(norm_factor, filters_ref, terms_ref, filter_ref, skip_ref, weight_ref):
    for row in range(0, filter_ref.shape[0], LANES):
        rows = pl.ds(row, LANES)
        total = sum((filters_ref[at, rows] for at in range(1, XS)), filters_ref[0, rows])
        filter_ref[rows, :] = total
        skip_ref[:, rows] = total.T[:1]
        total = sum(
            (terms_ref[at, rows].astype(F32) for at in range(1, ZL)),
            terms_ref[0, rows].astype(F32),
        )
        weight_ref[rows, :] = total * norm_factor


def call(kernel, name, shapes, scratch, flops, moved, vmem=32, **specs):
    return pl.pallas_call(
        kernel,
        out_shape=shapes,
        scratch_shapes=scratch,
        name=name,
        compiler_params=pltpu.CompilerParams(vmem_limit_bytes=vmem * 1024 * 1024),
        cost_estimate=pl.CostEstimate(flops=flops, bytes_accessed=moved, transcendentals=0),
        **specs,
    )


def body(grad_out, query_gate, key_gate, value_input, filter_taps, skip_gain, out_weight):
    rows, width = query_gate.shape
    norm_factor = 1.0 / math.sqrt(rows * lax.axis_size("seq"))
    gain = skip_gain.reshape(1, width)
    block_f32 = jax.ShapeDtypeStruct((rows, width), F32)
    block_bf16 = jax.ShapeDtypeStruct((rows, width), BF16)
    padded = pltpu.VMEM((2 * rows, width), F32)
    held_f32, held_bf16 = pltpu.VMEM((rows, width), F32), pltpu.VMEM((rows, width), BF16)
    held_rows = pltpu.VMEM((TAPS, LANES), F32)
    in_vmem = pl.BlockSpec(memory_space=pltpu.VMEM)
    in_hbm = pl.BlockSpec(memory_space=pltpu.HBM)
    stay = lambda value: pltpu.with_memory_space_constraint(value, pltpu.HBM)
    query, key, value = stay(query_gate), stay(key_gate), stay(value_input)
    weight = stay(out_weight)
    halves = width // LANES
    held_mixers = pltpu.VMEM((halves, LANES, rows), BF16)
    size = rows * width

    mixed_in = key_gate.astype(F32) * value_input.astype(F32)
    previous = passed_along(mixed_in, "seq", 1)
    over_zh = lax.all_gather(grad_out, "chan", axis=0, axis_index_groups=ZH_GROUPS)
    gathered = spread(over_zh, "chan", Y_GROUPS, YS)
    gathered = gathered.reshape(YS, ZH, rows, width)
    targets, blocks = ZH * CORES, YS + halves
    packed_out = pltpu.HBM((targets, blocks, rows, LANES), BF16)
    summed, packed = call(
        causal_kernel,
        "causal",
        (pltpu.HBM((rows, width), F32), packed_out),
        [
            padded,
            held_rows,
            held_bf16,
            held_f32,
            held_mixers,
            pltpu.SemaphoreType.DMA((2 + targets,)),
        ],
        2 * size * TAPS,
        20 * size,
        in_specs=[in_vmem, in_vmem, in_vmem, in_vmem, in_hbm],
        out_specs=[in_hbm, in_hbm],
    )(previous, mixed_in, filter_taps, gain, query)
    packed = call(
        pack_kernel,
        "pack",
        packed_out,
        [pltpu.SemaphoreType.DMA((targets, YS))],
        0,
        64 * size,
        in_specs=[in_vmem, in_hbm],
        out_specs=in_hbm,
        input_output_aliases={1: 0},
    )(gathered, stay(packed))
    pieces = exchange(packed, "seq", XC_GROUPS)

    grad_query, grad_sum, filter_term = call(
        lambda *refs: main_kernel(norm_factor, *refs),
        "main",
        (block_bf16, block_f32, jax.ShapeDtypeStruct((width, TAPS), F32)),
        [
            pltpu.VMEM((ZH, width, YS * width), BF16),
            held_bf16,
            held_f32,
            padded,
            held_rows,
            pltpu.SemaphoreType.DMA((ZH,)),
            pltpu.SemaphoreType.DMA((2,)),
        ],
        2 * size * (4096 + TAPS),
        4 * 1024 * 1024,
        in_specs=[in_vmem, in_hbm, in_hbm, in_hbm, in_vmem, in_vmem],
    )(gathered, weight, query, stay(summed), previous, mixed_in)
    incoming = passed_along(grad_sum, "seq", -1)
    filter_term = jnp.sum(collect(filter_term, CORE_GROUPS), axis=0)
    filter_term = (filter_term + other_z(filter_term, 1)).astype(BF16)
    filter_term = filter_term.astype(F32) + other_z(filter_term, 2).astype(F32)
    grad_key, grad_value = call(
        ahead_kernel,
        "ahead",
        (block_bf16, block_bf16),
        [
            padded,
            held_rows,
            held_bf16,
            held_bf16,
            pltpu.SemaphoreType.DMA((2,)),
        ],
        2 * size * TAPS,
        20 * size,
        in_specs=[in_vmem, in_vmem, in_vmem, in_vmem, in_hbm, in_hbm],
    )(grad_sum, incoming, filter_taps, gain, key, value)
    pieces, grad_key, grad_value = lax.optimization_barrier((pieces, grad_key, grad_value))
    partial = call(
        weight_kernel,
        "weight",
        jax.ShapeDtypeStruct((ZL, width, LANES), BF16),
        [],
        2 * XS * CORES * rows * width * ZL * LANES,
        2 * 1024 * 1024,
    )(pieces)
    partial, filter_term = lax.optimization_barrier((partial, filter_term))
    terms = exchange(partial, "seq", ZL_GROUPS)
    grad_filter, grad_skip, grad_weight = call(
        lambda *refs: finish_kernel(norm_factor, *refs),
        "finish",
        (
            jax.ShapeDtypeStruct((width, TAPS), F32),
            jax.ShapeDtypeStruct((1, width), F32),
            jax.ShapeDtypeStruct((width, LANES), F32),
        ),
        [],
        8 * size,
        32 * size,
    )(collect(filter_term, X_GROUPS), terms)
    grad_skip = grad_skip.reshape(width)
    return (grad_query, grad_key, grad_value, grad_filter, grad_skip, grad_weight)


def solution(mesh):
    return jax.shard_map(
        body,
        mesh=mesh,
        in_specs=(
            P("seq", "chan"),
            P("seq", "chan"),
            P("seq", "chan"),
            P("seq", "chan"),
            P("chan", None),
            P("chan"),
            P("chan", None),
        ),
        out_specs=(
            P("seq", "chan"),
            P("seq", "chan"),
            P("seq", "chan"),
            P("chan", None),
            P("chan"),
            P("chan", "seq"),
        ),
        check_vma=False,
    )
```

```python
import math

import jax
import jax.numpy as jnp
from jax import lax
from jax.experimental import pallas as pl
from jax.experimental.pallas import tpu as pltpu
from jax.sharding import PartitionSpec as P

TAPS = 128
LANES = 128
SUB = 8
XS, ZL, CORES = 4, 4, 2
ZH, YS = 4, 4
F32 = jnp.float32
BF16 = jnp.bfloat16


def seq_index(x, zl, core):
    return (x * ZL + zl) * CORES + core


def chan_index(zh, y):
    return zh * YS + y


ZH_GROUPS = [[chan_index(zh, y) for zh in range(ZH)] for y in range(YS)]
Y_GROUPS = [[chan_index(zh, y) for y in range(YS)] for zh in range(ZH)]
XC_GROUPS = [
    [seq_index(x, zl, core) for x in range(XS) for core in range(CORES)] for zl in range(ZL)
]
ZL_GROUPS = [
    [seq_index(x, zl, core) for zl in range(ZL)] for x in range(XS) for core in range(CORES)
]
X_GROUPS = [
    [seq_index(x, zl, core) for x in range(XS)] for zl in range(ZL) for core in range(CORES)
]
CORE_GROUPS = [
    [seq_index(x, zl, core) for core in range(CORES)] for x in range(XS) for zl in range(ZL)
]


def exchange(value, axis, groups):
    return lax.all_to_all(value, axis, 0, 0, tiled=True, axis_index_groups=groups)


def spread(value, axis, groups, size):
    return exchange(jnp.broadcast_to(value[None], (size, *value.shape)), axis, groups)


def collect(value, groups):
    return lax.all_gather(value, "seq", axis=0, axis_index_groups=groups)


def other_z(value, flip):
    pairs = [
        (seq_index(x, zl, core), seq_index(x, zl ^ flip, core))
        for x in range(XS)
        for zl in range(ZL)
        for core in range(CORES)
    ]
    return lax.ppermute(value, "seq", pairs)


def passed_along(value, axis, by):
    size = lax.axis_size(axis)
    pairs = [(i, i + by) for i in range(size) if 0 <= i + by < size]
    return lax.ppermute(value, axis, pairs)


def fetch(sources, held, sem, first=0):
    copies = [
        pltpu.make_async_copy(source, target, sem.at[first + at])
        for at, (source, target) in enumerate(zip(sources, held))
    ]
    for copy in copies:
        copy.start()
    return copies


def finish(copies):
    for copy in copies:
        copy.wait()


def weighted(shifted, tap_rows, starts, rows):
    part = None
    for tap, start in starts:
        term = tap_rows[tap : tap + 1, :] * shifted[start : start + rows]
        part = term if part is None else part + term
    return part


def causal_kernel(
    prev_ref,
    mixed_ref,
    taps_ref,
    gain_ref,
    query_ref,
    summed_ref,
    packed_ref,
    pad,
    tap_rows,
    query,
    summed,
    mixers,
    sem,
):
    copies = fetch((query_ref,), (query,), sem)
    rows, width = mixed_ref.shape
    pad[:rows] = prev_ref[...]
    pad[rows:] = mixed_ref[...]
    for lane in range(0, width, LANES):
        cols = pl.ds(lane, LANES)
        tap_rows[...] = taps_ref[cols, :].T
        total = gain_ref[:, cols] * mixed_ref[:, cols]
        for r in range(SUB):
            shifted = pad[pl.ds(SUB - r, 2 * rows - SUB), cols]
            starts = [(SUB * q + r, rows - SUB - SUB * q) for q in range(TAPS // SUB)]
            total = total + weighted(shifted, tap_rows, starts, rows)
        summed[:, cols] = total
        if lane == 0:
            finish(copies)
        mixers[lane // LANES] = (query[:, cols].astype(F32) * total).T.astype(BF16)
    targets, halves = packed_ref.shape[0], mixers.shape[0]
    places = [packed_ref.at[target, pl.ds(YS, halves)] for target in range(targets)]
    finish(fetch([summed] + [mixers] * targets, [summed_ref] + places, sem, 1))


def pack_kernel(gathered_ref, begun_ref, packed_ref, sem):
    del begun_ref
    targets = [(zh, core) for zh in range(ZH) for core in range(CORES)]
    sources = [gathered_ref.at[:, zh, :, pl.ds(core * LANES, LANES)] for zh, core in targets]
    places = [packed_ref.at[zh * CORES + core, pl.ds(0, YS)] for zh, core in targets]
    finish(fetch(sources, places, sem))


def main_kernel(
    norm_factor,
    gathered_ref,
    weight_ref,
    query_ref,
    summed_ref,
    prev_ref,
    mixed_ref,
    grad_query_ref,
    grad_sum_ref,
    filter_ref,
    held,
    query,
    summed,
    pad,
    tap_rows,
    weight_sem,
    sem,
):
    rows, width = mixed_ref.shape
    loads = []
    for zh in range(ZH):
        cols = pl.ds(zh * YS * width, YS * width)
        loads.append(pltpu.make_async_copy(weight_ref.at[:, cols], held.at[zh], weight_sem.at[zh]))
        loads[-1].start()
    blocks = fetch((query_ref, summed_ref), (query, summed), sem)
    pad[:rows] = prev_ref[...]
    pad[rows:] = mixed_ref[...]

    total = None
    for zh in range(ZH):
        loads[zh].wait()
        for y in range(YS):
            term = lax.dot_general(
                gathered_ref[y, zh],
                held[zh, :, pl.ds(y * width, width)],
                (((1,), (1,)), ((), ())),
                preferred_element_type=F32,
            )
            total = term if total is None else total + term
    finish(blocks)
    grad_query_ref[...] = (total * summed[...]).astype(BF16)
    grad_sum_ref[...] = total * query[...].astype(F32)

    for lane in range(0, width, LANES):
        cols = pl.ds(lane, LANES)
        grad_sum = grad_sum_ref[:, cols]
        for r in range(SUB):
            shifted = pad[pl.ds(SUB - r, 2 * rows - SUB), cols]
            for q in range(TAPS // SUB):
                start = rows - SUB - SUB * q
                j = SUB * q + r
                tap_rows[j : j + 1, :] = jnp.sum(
                    grad_sum * shifted[start : start + rows], axis=0, keepdims=True
                )
        filter_ref[cols, :] = tap_rows[...].T * norm_factor


def ahead_kernel(
    grad_sum_ref,
    incoming_ref,
    taps_ref,
    gain_ref,
    key_ref,
    value_ref,
    grad_key_ref,
    grad_value_ref,
    pad,
    tap_rows,
    key,
    value,
    sem,
):
    copies = fetch((key_ref, value_ref), (key, value), sem)
    rows, width = grad_sum_ref.shape
    pad[:rows] = grad_sum_ref[...]
    pad[rows:] = incoming_ref[...]
    for lane in range(0, width, LANES):
        cols = pl.ds(lane, LANES)
        tap_rows[...] = taps_ref[cols, :].T
        total = gain_ref[:, cols] * grad_sum_ref[:, cols]
        for r in range(SUB):
            shifted = pad[pl.ds(r, 2 * rows - SUB), cols]
            starts = [(SUB * q + r, SUB * q) for q in range(TAPS // SUB)]
            total = total + weighted(shifted, tap_rows, starts, rows)
        if lane == 0:
            finish(copies)
        grad_key_ref[:, cols] = (total * value[:, cols].astype(F32)).astype(BF16)
        grad_value_ref[:, cols] = (total * key[:, cols].astype(F32)).astype(BF16)


def weight_kernel(pieces_ref, out_ref):
    def side_by_side(blocks):
        return jnp.concatenate(blocks, axis=1)

    halves = pieces_ref.shape[1] - ZL
    for pair in range(0, ZL, 2):
        total = None
        for x in range(XS):
            sources = range(CORES * x, CORES * (x + 1))
            mixers = jnp.concatenate(
                [side_by_side([pieces_ref[at, ZL + half] for at in sources]) for half in range(halves)],
                axis=0,
            )
            tokens = jnp.concatenate(
                [side_by_side([pieces_ref[at, pair + k] for k in range(2)]) for at in sources], axis=0
            )
            term = jnp.dot(mixers, tokens, preferred_element_type=F32)
            total = term if total is None else total + term
        for k in range(2):
            out_ref[pair + k] = total[:, k * LANES : (k + 1) * LANES].astype(BF16)


def finish_kernel(norm_factor, filters_ref, terms_ref, filter_ref, skip_ref, weight_ref):
    for row in range(0, filter_ref.shape[0], LANES):
        rows = pl.ds(row, LANES)
        total = sum((filters_ref[at, rows] for at in range(1, XS)), filters_ref[0, rows])
        filter_ref[rows, :] = total
        skip_ref[:, rows] = total.T[:1]
        total = sum(
            (terms_ref[at, rows].astype(F32) for at in range(1, ZL)),
            terms_ref[0, rows].astype(F32),
        )
        weight_ref[rows, :] = total * norm_factor


def call(kernel, name, shapes, scratch, flops, moved, vmem=32, **specs):
    return pl.pallas_call(
        kernel,
        out_shape=shapes,
        scratch_shapes=scratch,
        name=name,
        compiler_params=pltpu.CompilerParams(vmem_limit_bytes=vmem * 1024 * 1024),
        cost_estimate=pl.CostEstimate(flops=flops, bytes_accessed=moved, transcendentals=0),
        **specs,
    )


def body(grad_out, query_gate, key_gate, value_input, filter_taps, skip_gain, out_weight):
    rows, width = query_gate.shape
    norm_factor = 1.0 / math.sqrt(rows * lax.axis_size("seq"))
    gain = skip_gain.reshape(1, width)
    block_f32 = jax.ShapeDtypeStruct((rows, width), F32)
    block_bf16 = jax.ShapeDtypeStruct((rows, width), BF16)
    padded = pltpu.VMEM((2 * rows, width), F32)
    held_f32, held_bf16 = pltpu.VMEM((rows, width), F32), pltpu.VMEM((rows, width), BF16)
    held_rows = pltpu.VMEM((TAPS, LANES), F32)
    in_vmem = pl.BlockSpec(memory_space=pltpu.VMEM)
    in_hbm = pl.BlockSpec(memory_space=pltpu.HBM)
    stay = lambda value: pltpu.with_memory_space_constraint(value, pltpu.HBM)
    query, key, value = stay(query_gate), stay(key_gate), stay(value_input)
    weight = stay(out_weight)
    halves = width // LANES
    held_mixers = pltpu.VMEM((halves, LANES, rows), BF16)
    size = rows * width

    mixed_in = key_gate.astype(F32) * value_input.astype(F32)
    previous = passed_along(mixed_in, "seq", 1)
    over_zh = lax.all_gather(grad_out, "chan", axis=0, axis_index_groups=ZH_GROUPS)
    gathered = spread(over_zh, "chan", Y_GROUPS, YS)
    gathered = gathered.reshape(YS, ZH, rows, width)
    targets, blocks = ZH * CORES, YS + halves
    packed_out = pltpu.HBM((targets, blocks, rows, LANES), BF16)
    summed, packed = call(
        causal_kernel,
        "causal",
        (pltpu.HBM((rows, width), F32), packed_out),
        [
            padded,
            held_rows,
            held_bf16,
            held_f32,
            held_mixers,
            pltpu.SemaphoreType.DMA((2 + targets,)),
        ],
        2 * size * TAPS,
        20 * size,
        in_specs=[in_vmem, in_vmem, in_vmem, in_vmem, in_hbm],
        out_specs=[in_hbm, in_hbm],
    )(previous, mixed_in, filter_taps, gain, query)
    packed = call(
        pack_kernel,
        "pack",
        packed_out,
        [pltpu.SemaphoreType.DMA((targets,))],
        0,
        64 * size,
        in_specs=[in_vmem, in_hbm],
        out_specs=in_hbm,
        input_output_aliases={1: 0},
    )(gathered, stay(packed))
    pieces = exchange(packed, "seq", XC_GROUPS)

    grad_query, grad_sum, filter_term = call(
        lambda *refs: main_kernel(norm_factor, *refs),
        "main",
        (block_bf16, block_f32, jax.ShapeDtypeStruct((width, TAPS), F32)),
        [
            pltpu.VMEM((ZH, width, YS * width), BF16),
            held_bf16,
            held_f32,
            padded,
            held_rows,
            pltpu.SemaphoreType.DMA((ZH,)),
            pltpu.SemaphoreType.DMA((2,)),
        ],
        2 * size * (4096 + TAPS),
        4 * 1024 * 1024,
        in_specs=[in_vmem, in_hbm, in_hbm, in_hbm, in_vmem, in_vmem],
    )(gathered, weight, query, stay(summed), previous, mixed_in)
    incoming = passed_along(grad_sum, "seq", -1)
    filter_term = jnp.sum(collect(filter_term, CORE_GROUPS), axis=0)
    filter_term = (filter_term + other_z(filter_term, 1)).astype(BF16)
    from_z = other_z(filter_term, 2)
    grad_key, grad_value = call(
        ahead_kernel,
        "ahead",
        (block_bf16, block_bf16),
        [
            padded,
            held_rows,
            held_bf16,
            held_bf16,
            pltpu.SemaphoreType.DMA((2,)),
        ],
        2 * size * TAPS,
        20 * size,
        in_specs=[in_vmem, in_vmem, in_vmem, in_vmem, in_hbm, in_hbm],
    )(grad_sum, incoming, filter_taps, gain, key, value)
    pieces, grad_key, grad_value = lax.optimization_barrier((pieces, grad_key, grad_value))
    partial = call(
        weight_kernel,
        "weight",
        jax.ShapeDtypeStruct((ZL, width, LANES), BF16),
        [],
        2 * XS * CORES * rows * width * ZL * LANES,
        2 * 1024 * 1024,
    )(pieces)
    partial, filter_term = lax.optimization_barrier((partial, filter_term))
    filter_term = filter_term.astype(F32) + from_z.astype(F32)
    partial, filter_term = lax.optimization_barrier((partial, filter_term))
    terms = exchange(partial, "seq", ZL_GROUPS)
    grad_filter, grad_skip, grad_weight = call(
        lambda *refs: finish_kernel(norm_factor, *refs),
        "finish",
        (
            jax.ShapeDtypeStruct((width, TAPS), F32),
            jax.ShapeDtypeStruct((1, width), F32),
            jax.ShapeDtypeStruct((width, LANES), F32),
        ),
        [],
        8 * size,
        32 * size,
    )(collect(filter_term, X_GROUPS), terms)
    grad_skip = grad_skip.reshape(width)
    return (grad_query, grad_key, grad_value, grad_filter, grad_skip, grad_weight)


def solution(mesh):
    return jax.shard_map(
        body,
        mesh=mesh,
        in_specs=(
            P("seq", "chan"),
            P("seq", "chan"),
            P("seq", "chan"),
            P("seq", "chan"),
            P("chan", None),
            P("chan"),
            P("chan", None),
        ),
        out_specs=(
            P("seq", "chan"),
            P("seq", "chan"),
            P("seq", "chan"),
            P("chan", None),
            P("chan"),
            P("chan", "seq"),
        ),
        check_vma=False,
    )
```

```python
import math

import jax
import jax.numpy as jnp
from jax import lax
from jax.experimental import pallas as pl
from jax.experimental.pallas import tpu as pltpu
from jax.sharding import PartitionSpec as P

TAPS = 128
LANES = 128
SUB = 8
XS, ZL, CORES = 4, 4, 2
ZH, YS = 4, 4
F32 = jnp.float32
BF16 = jnp.bfloat16


def seq_index(x, zl, core):
    return (x * ZL + zl) * CORES + core


def chan_index(zh, y):
    return zh * YS + y


ZH_GROUPS = [[chan_index(zh, y) for zh in range(ZH)] for y in range(YS)]
Y_GROUPS = [[chan_index(zh, y) for y in range(YS)] for zh in range(ZH)]
XC_GROUPS = [
    [seq_index(x, zl, core) for x in range(XS) for core in range(CORES)] for zl in range(ZL)
]
ZL_GROUPS = [
    [seq_index(x, zl, core) for zl in range(ZL)] for x in range(XS) for core in range(CORES)
]
X_PAIRS = [
    [seq_index(x + half, zl, core) for half in (0, XS // 2)]
    for x in range(XS // 2)
    for zl in range(ZL)
    for core in range(CORES)
]
CORE_GROUPS = [
    [seq_index(x, zl, core) for core in range(CORES)] for x in range(XS) for zl in range(ZL)
]


def exchange(value, axis, groups):
    return lax.all_to_all(value, axis, 0, 0, tiled=True, axis_index_groups=groups)


def spread(value, axis, groups, size):
    return exchange(jnp.broadcast_to(value[None], (size, *value.shape)), axis, groups)


def collect(value, groups):
    return lax.all_gather(value, "seq", axis=0, axis_index_groups=groups)


def swapped(value, flip_x, flip_z):
    pairs = [
        (seq_index(x, zl, core), seq_index(x ^ flip_x, zl ^ flip_z, core))
        for x in range(XS)
        for zl in range(ZL)
        for core in range(CORES)
    ]
    return lax.ppermute(value, "seq", pairs)


def passed_along(value, axis, by):
    size = lax.axis_size(axis)
    pairs = [(i, i + by) for i in range(size) if 0 <= i + by < size]
    return lax.ppermute(value, axis, pairs)


def fetch(sources, held, sem, first=0):
    copies = [
        pltpu.make_async_copy(source, target, sem.at[first + at])
        for at, (source, target) in enumerate(zip(sources, held))
    ]
    for copy in copies:
        copy.start()
    return copies


def finish(copies):
    for copy in copies:
        copy.wait()


def weighted(shifted, tap_rows, starts, rows):
    part = None
    for tap, start in starts:
        term = tap_rows[tap : tap + 1, :] * shifted[start : start + rows]
        part = term if part is None else part + term
    return part


def causal_kernel(
    prev_ref,
    mixed_ref,
    taps_ref,
    gain_ref,
    query_ref,
    summed_ref,
    packed_ref,
    pad,
    tap_rows,
    query,
    summed,
    mixers,
    sem,
):
    copies = fetch((query_ref,), (query,), sem)
    rows, width = mixed_ref.shape
    pad[:rows] = prev_ref[...]
    pad[rows:] = mixed_ref[...]
    for lane in range(0, width, LANES):
        cols = pl.ds(lane, LANES)
        tap_rows[...] = taps_ref[cols, :].T
        total = gain_ref[:, cols] * mixed_ref[:, cols]
        for r in range(SUB):
            shifted = pad[pl.ds(SUB - r, 2 * rows - SUB), cols]
            starts = [(SUB * q + r, rows - SUB - SUB * q) for q in range(TAPS // SUB)]
            total = total + weighted(shifted, tap_rows, starts, rows)
        summed[:, cols] = total
        if lane == 0:
            finish(copies)
        mixers[lane // LANES] = (query[:, cols].astype(F32) * total).T.astype(BF16)
    targets, halves = packed_ref.shape[0], mixers.shape[0]
    places = [packed_ref.at[target, pl.ds(YS, halves)] for target in range(targets)]
    finish(fetch([summed] + [mixers] * targets, [summed_ref] + places, sem, 1))


def pack_kernel(gathered_ref, begun_ref, packed_ref, sem):
    del begun_ref
    targets = [(zh, core) for zh in range(ZH) for core in range(CORES)]
    sources = [gathered_ref.at[:, zh, :, pl.ds(core * LANES, LANES)] for zh, core in targets]
    places = [packed_ref.at[zh * CORES + core, pl.ds(0, YS)] for zh, core in targets]
    finish(fetch(sources, places, sem))


def main_kernel(
    norm_factor,
    gathered_ref,
    weight_ref,
    query_ref,
    summed_ref,
    prev_ref,
    mixed_ref,
    grad_query_ref,
    grad_sum_ref,
    filter_ref,
    held,
    query,
    summed,
    pad,
    tap_rows,
    weight_sem,
    sem,
):
    rows, width = mixed_ref.shape
    loads = []
    for zh in range(ZH):
        cols = pl.ds(zh * YS * width, YS * width)
        loads.append(pltpu.make_async_copy(weight_ref.at[:, cols], held.at[zh], weight_sem.at[zh]))
        loads[-1].start()
    blocks = fetch((query_ref, summed_ref), (query, summed), sem)
    pad[:rows] = prev_ref[...]
    pad[rows:] = mixed_ref[...]

    total = None
    for zh in range(ZH):
        loads[zh].wait()
        for y in range(YS):
            term = lax.dot_general(
                gathered_ref[y, zh],
                held[zh, :, pl.ds(y * width, width)],
                (((1,), (1,)), ((), ())),
                preferred_element_type=F32,
            )
            total = term if total is None else total + term
    finish(blocks)
    grad_query_ref[...] = (total * summed[...]).astype(BF16)
    grad_sum_ref[...] = total * query[...].astype(F32)

    for lane in range(0, width, LANES):
        cols = pl.ds(lane, LANES)
        grad_sum = grad_sum_ref[:, cols]
        for r in range(SUB):
            shifted = pad[pl.ds(SUB - r, 2 * rows - SUB), cols]
            for q in range(TAPS // SUB):
                start = rows - SUB - SUB * q
                j = SUB * q + r
                tap_rows[j : j + 1, :] = jnp.sum(
                    grad_sum * shifted[start : start + rows], axis=0, keepdims=True
                )
        filter_ref[cols, :] = tap_rows[...].T * norm_factor


def ahead_kernel(
    grad_sum_ref,
    incoming_ref,
    taps_ref,
    gain_ref,
    key_ref,
    value_ref,
    grad_key_ref,
    grad_value_ref,
    pad,
    tap_rows,
    key,
    value,
    sem,
):
    copies = fetch((key_ref, value_ref), (key, value), sem)
    rows, width = grad_sum_ref.shape
    pad[:rows] = grad_sum_ref[...]
    pad[rows:] = incoming_ref[...]
    for lane in range(0, width, LANES):
        cols = pl.ds(lane, LANES)
        tap_rows[...] = taps_ref[cols, :].T
        total = gain_ref[:, cols] * grad_sum_ref[:, cols]
        for r in range(SUB):
            shifted = pad[pl.ds(r, 2 * rows - SUB), cols]
            starts = [(SUB * q + r, SUB * q) for q in range(TAPS // SUB)]
            total = total + weighted(shifted, tap_rows, starts, rows)
        if lane == 0:
            finish(copies)
        grad_key_ref[:, cols] = (total * value[:, cols].astype(F32)).astype(BF16)
        grad_value_ref[:, cols] = (total * key[:, cols].astype(F32)).astype(BF16)


def weight_kernel(pieces_ref, out_ref):
    def side_by_side(blocks):
        return jnp.concatenate(blocks, axis=1)

    halves = pieces_ref.shape[1] - ZL
    for pair in range(0, ZL, 2):
        total = None
        for x in range(XS):
            sources = range(CORES * x, CORES * (x + 1))
            mixers = jnp.concatenate(
                [side_by_side([pieces_ref[at, ZL + half] for at in sources]) for half in range(halves)],
                axis=0,
            )
            tokens = jnp.concatenate(
                [side_by_side([pieces_ref[at, pair + k] for k in range(2)]) for at in sources], axis=0
            )
            term = jnp.dot(mixers, tokens, preferred_element_type=F32)
            total = term if total is None else total + term
        for k in range(2):
            out_ref[pair + k] = total[:, k * LANES : (k + 1) * LANES].astype(BF16)


def filter_kernel(both_ref, filter_ref, skip_ref):
    for row in range(0, filter_ref.shape[0], LANES):
        rows = pl.ds(row, LANES)
        total = both_ref[0, rows] + both_ref[1, rows]
        filter_ref[rows, :] = total
        skip_ref[:, rows] = total.T[:1]


def call(kernel, name, shapes, scratch, flops, moved, vmem=32, **specs):
    return pl.pallas_call(
        kernel,
        out_shape=shapes,
        scratch_shapes=scratch,
        name=name,
        compiler_params=pltpu.CompilerParams(vmem_limit_bytes=vmem * 1024 * 1024),
        cost_estimate=pl.CostEstimate(flops=flops, bytes_accessed=moved, transcendentals=0),
        **specs,
    )


def body(grad_out, query_gate, key_gate, value_input, filter_taps, skip_gain, out_weight):
    rows, width = query_gate.shape
    norm_factor = 1.0 / math.sqrt(rows * lax.axis_size("seq"))
    gain = skip_gain.reshape(1, width)
    block_f32 = jax.ShapeDtypeStruct((rows, width), F32)
    block_bf16 = jax.ShapeDtypeStruct((rows, width), BF16)
    padded = pltpu.VMEM((2 * rows, width), F32)
    held_f32, held_bf16 = pltpu.VMEM((rows, width), F32), pltpu.VMEM((rows, width), BF16)
    held_rows = pltpu.VMEM((TAPS, LANES), F32)
    in_vmem = pl.BlockSpec(memory_space=pltpu.VMEM)
    in_hbm = pl.BlockSpec(memory_space=pltpu.HBM)
    stay = lambda value: pltpu.with_memory_space_constraint(value, pltpu.HBM)
    query, key, value = stay(query_gate), stay(key_gate), stay(value_input)
    weight = stay(out_weight)
    halves = width // LANES
    held_mixers = pltpu.VMEM((halves, LANES, rows), BF16)
    size = rows * width

    mixed_in = key_gate.astype(F32) * value_input.astype(F32)
    previous = passed_along(mixed_in, "seq", 1)
    over_zh = lax.all_gather(grad_out, "chan", axis=0, axis_index_groups=ZH_GROUPS)
    gathered = spread(over_zh, "chan", Y_GROUPS, YS)
    gathered = gathered.reshape(YS, ZH, rows, width)
    targets, blocks = ZH * CORES, YS + halves
    packed_out = pltpu.HBM((targets, blocks, rows, LANES), BF16)
    summed, packed = call(
        causal_kernel,
        "causal",
        (pltpu.HBM((rows, width), F32), packed_out),
        [
            padded,
            held_rows,
            held_bf16,
            held_f32,
            held_mixers,
            pltpu.SemaphoreType.DMA((2 + targets,)),
        ],
        2 * size * TAPS,
        20 * size,
        in_specs=[in_vmem, in_vmem, in_vmem, in_vmem, in_hbm],
        out_specs=[in_hbm, in_hbm],
    )(previous, mixed_in, filter_taps, gain, query)
    packed = call(
        pack_kernel,
        "pack",
        packed_out,
        [pltpu.SemaphoreType.DMA((targets,))],
        0,
        64 * size,
        in_specs=[in_vmem, in_hbm],
        out_specs=in_hbm,
        input_output_aliases={1: 0},
    )(gathered, stay(packed))
    pieces = exchange(packed, "seq", XC_GROUPS)

    grad_query, grad_sum, filter_term = call(
        lambda *refs: main_kernel(norm_factor, *refs),
        "main",
        (block_bf16, block_f32, jax.ShapeDtypeStruct((width, TAPS), F32)),
        [
            pltpu.VMEM((ZH, width, YS * width), BF16),
            held_bf16,
            held_f32,
            padded,
            held_rows,
            pltpu.SemaphoreType.DMA((ZH,)),
            pltpu.SemaphoreType.DMA((2,)),
        ],
        2 * size * (4096 + TAPS),
        4 * 1024 * 1024,
        in_specs=[in_vmem, in_hbm, in_hbm, in_hbm, in_vmem, in_vmem],
    )(gathered, weight, query, stay(summed), previous, mixed_in)
    incoming = passed_along(grad_sum, "seq", -1)
    filter_term = jnp.sum(collect(filter_term, CORE_GROUPS), axis=0)
    filter_term = (filter_term + swapped(filter_term, 0, 1)).astype(BF16)
    from_z = swapped(filter_term, 0, 2)
    grad_key, grad_value = call(
        ahead_kernel,
        "ahead",
        (block_bf16, block_bf16),
        [
            padded,
            held_rows,
            held_bf16,
            held_bf16,
            pltpu.SemaphoreType.DMA((2,)),
        ],
        2 * size * TAPS,
        20 * size,
        in_specs=[in_vmem, in_vmem, in_vmem, in_vmem, in_hbm, in_hbm],
    )(grad_sum, incoming, filter_taps, gain, key, value)
    pieces, grad_key, grad_value = lax.optimization_barrier((pieces, grad_key, grad_value))
    partial = call(
        weight_kernel,
        "weight",
        jax.ShapeDtypeStruct((ZL, width, LANES), BF16),
        [],
        2 * XS * CORES * rows * width * ZL * LANES,
        2 * 1024 * 1024,
    )(pieces)
    partial, filter_term = lax.optimization_barrier((partial, filter_term))
    filter_term = filter_term.astype(F32) + from_z.astype(F32)
    partial, filter_term = lax.optimization_barrier((partial, filter_term))
    from_x = swapped(filter_term, 1, 0)
    terms = exchange(partial, "seq", ZL_GROUPS)
    grad_filter, grad_skip = call(
        filter_kernel,
        "filter",
        (jax.ShapeDtypeStruct((width, TAPS), F32), jax.ShapeDtypeStruct((1, width), F32)),
        [],
        1 << 36,
        1 << 28,
    )(collect(filter_term + from_x, X_PAIRS))
    terms, grad_filter, grad_skip = lax.optimization_barrier((terms, grad_filter, grad_skip))
    grad_skip = grad_skip.reshape(width)
    grad_weight = jnp.sum(terms.astype(F32), axis=0) * norm_factor
    return (grad_query, grad_key, grad_value, grad_filter, grad_skip, grad_weight)


def solution(mesh):
    return jax.shard_map(
        body,
        mesh=mesh,
        in_specs=(
            P("seq", "chan"),
            P("seq", "chan"),
            P("seq", "chan"),
            P("seq", "chan"),
            P("chan", None),
            P("chan"),
            P("chan", None),
        ),
        out_specs=(
            P("seq", "chan"),
            P("seq", "chan"),
            P("seq", "chan"),
            P("chan", None),
            P("chan"),
            P("chan", "seq"),
        ),
        check_vma=False,
    )
```

```python
import math

import jax
import jax.numpy as jnp
from jax import lax
from jax.experimental import pallas as pl
from jax.experimental.pallas import tpu as pltpu
from jax.sharding import PartitionSpec as P

TAPS = 128
LANES = 128
SUB = 8
XS, ZL, CORES = 4, 4, 2
ZH, YS = 4, 4
F32 = jnp.float32
BF16 = jnp.bfloat16


def seq_index(x, zl, core):
    return (x * ZL + zl) * CORES + core


def chan_index(zh, y):
    return zh * YS + y


ZH_GROUPS = [[chan_index(zh, y) for zh in range(ZH)] for y in range(YS)]
Y_GROUPS = [[chan_index(zh, y) for y in range(YS)] for zh in range(ZH)]
XC_GROUPS = [
    [seq_index(x, zl, core) for x in range(XS) for core in range(CORES)] for zl in range(ZL)
]
ZL_GROUPS = [
    [seq_index(x, zl, core) for zl in range(ZL)] for x in range(XS) for core in range(CORES)
]
X_PAIRS = [
    [seq_index(x + half, zl, core) for half in (0, XS // 2)]
    for x in range(XS // 2)
    for zl in range(ZL)
    for core in range(CORES)
]
CORE_GROUPS = [
    [seq_index(x, zl, core) for core in range(CORES)] for x in range(XS) for zl in range(ZL)
]


def exchange(value, axis, groups):
    return lax.all_to_all(value, axis, 0, 0, tiled=True, axis_index_groups=groups)


def spread(value, axis, groups, size):
    return exchange(jnp.broadcast_to(value[None], (size, *value.shape)), axis, groups)


def collect(value, groups):
    return lax.all_gather(value, "seq", axis=0, axis_index_groups=groups)


def swapped(value, flip_x, flip_z):
    pairs = [
        (seq_index(x, zl, core), seq_index(x ^ flip_x, zl ^ flip_z, core))
        for x in range(XS)
        for zl in range(ZL)
        for core in range(CORES)
    ]
    return lax.ppermute(value, "seq", pairs)


def passed_along(value, axis, by):
    size = lax.axis_size(axis)
    pairs = [(i, i + by) for i in range(size) if 0 <= i + by < size]
    return lax.ppermute(value, axis, pairs)


def fetch(sources, held, sem, first=0):
    copies = [
        pltpu.make_async_copy(source, target, sem.at[first + at])
        for at, (source, target) in enumerate(zip(sources, held))
    ]
    for copy in copies:
        copy.start()
    return copies


def finish(copies):
    for copy in copies:
        copy.wait()


def weighted(shifted, tap_rows, starts, rows):
    part = None
    for tap, start in starts:
        term = tap_rows[tap : tap + 1, :] * shifted[start : start + rows]
        part = term if part is None else part + term
    return part


def causal_kernel(
    prev_ref,
    mixed_ref,
    taps_ref,
    gain_ref,
    query_ref,
    summed_ref,
    packed_ref,
    pad,
    tap_rows,
    query,
    summed,
    mixers,
    sem,
):
    copies = fetch((query_ref,), (query,), sem)
    stores = []
    rows, width = mixed_ref.shape
    pad[:rows] = prev_ref[...]
    pad[rows:] = mixed_ref[...]
    for lane in range(0, width, LANES):
        cols = pl.ds(lane, LANES)
        tap_rows[...] = taps_ref[cols, :].T
        total = gain_ref[:, cols] * mixed_ref[:, cols]
        for r in range(SUB):
            shifted = pad[pl.ds(SUB - r, 2 * rows - SUB), cols]
            starts = [(SUB * q + r, rows - SUB - SUB * q) for q in range(TAPS // SUB)]
            total = total + weighted(shifted, tap_rows, starts, rows)
        summed[:, cols] = total
        stores += fetch((summed.at[:, cols],), (summed_ref.at[:, cols],), sem, 1 + lane // LANES)
        if lane == 0:
            finish(copies)
        mixers[lane // LANES] = (query[:, cols].astype(F32) * total).T.astype(BF16)
    targets, halves = packed_ref.shape[0], mixers.shape[0]
    places = [packed_ref.at[target, pl.ds(YS, halves)] for target in range(targets)]
    finish(stores + fetch([mixers] * targets, places, sem, 1 + halves))


def pack_kernel(gathered_ref, begun_ref, packed_ref, sem):
    del begun_ref
    targets = [(zh, core) for zh in range(ZH) for core in range(CORES)]
    sources = [gathered_ref.at[:, zh, :, pl.ds(core * LANES, LANES)] for zh, core in targets]
    places = [packed_ref.at[zh * CORES + core, pl.ds(0, YS)] for zh, core in targets]
    finish(fetch(sources, places, sem))


def main_kernel(
    norm_factor,
    gathered_ref,
    weight_ref,
    query_ref,
    summed_ref,
    prev_ref,
    mixed_ref,
    grad_query_ref,
    grad_sum_ref,
    filter_ref,
    held,
    query,
    summed,
    pad,
    tap_rows,
    weight_sem,
    sem,
):
    rows, width = mixed_ref.shape
    loads = []
    for zh in range(ZH):
        cols = pl.ds(zh * YS * width, YS * width)
        loads.append(pltpu.make_async_copy(weight_ref.at[:, cols], held.at[zh], weight_sem.at[zh]))
        loads[-1].start()
    blocks = fetch((query_ref, summed_ref), (query, summed), sem)
    pad[:rows] = prev_ref[...]
    pad[rows:] = mixed_ref[...]

    total = None
    for zh in range(ZH):
        loads[zh].wait()
        for y in range(YS):
            term = lax.dot_general(
                gathered_ref[y, zh],
                held[zh, :, pl.ds(y * width, width)],
                (((1,), (1,)), ((), ())),
                preferred_element_type=F32,
            )
            total = term if total is None else total + term
    finish(blocks)
    grad_query_ref[...] = (total * summed[...]).astype(BF16)
    grad_sum_ref[...] = total * query[...].astype(F32)

    for lane in range(0, width, LANES):
        cols = pl.ds(lane, LANES)
        grad_sum = grad_sum_ref[:, cols]
        for r in range(SUB):
            shifted = pad[pl.ds(SUB - r, 2 * rows - SUB), cols]
            for q in range(TAPS // SUB):
                start = rows - SUB - SUB * q
                j = SUB * q + r
                tap_rows[j : j + 1, :] = jnp.sum(
                    grad_sum * shifted[start : start + rows], axis=0, keepdims=True
                )
        filter_ref[cols, :] = tap_rows[...].T * norm_factor


def ahead_kernel(
    grad_sum_ref,
    incoming_ref,
    taps_ref,
    gain_ref,
    key_ref,
    value_ref,
    grad_key_ref,
    grad_value_ref,
    pad,
    tap_rows,
    key,
    value,
    sem,
):
    copies = fetch((key_ref, value_ref), (key, value), sem)
    rows, width = grad_sum_ref.shape
    pad[:rows] = grad_sum_ref[...]
    pad[rows:] = incoming_ref[...]
    for lane in range(0, width, LANES):
        cols = pl.ds(lane, LANES)
        tap_rows[...] = taps_ref[cols, :].T
        total = gain_ref[:, cols] * grad_sum_ref[:, cols]
        for r in range(SUB):
            shifted = pad[pl.ds(r, 2 * rows - SUB), cols]
            starts = [(SUB * q + r, SUB * q) for q in range(TAPS // SUB)]
            total = total + weighted(shifted, tap_rows, starts, rows)
        if lane == 0:
            finish(copies)
        grad_key_ref[:, cols] = (total * value[:, cols].astype(F32)).astype(BF16)
        grad_value_ref[:, cols] = (total * key[:, cols].astype(F32)).astype(BF16)


def weight_kernel(pieces_ref, out_ref):
    def side_by_side(blocks):
        return jnp.concatenate(blocks, axis=1)

    halves = pieces_ref.shape[1] - ZL
    for pair in range(0, ZL, 2):
        total = None
        for x in range(XS):
            sources = range(CORES * x, CORES * (x + 1))
            mixers = jnp.concatenate(
                [side_by_side([pieces_ref[at, ZL + half] for at in sources]) for half in range(halves)],
                axis=0,
            )
            tokens = jnp.concatenate(
                [side_by_side([pieces_ref[at, pair + k] for k in range(2)]) for at in sources], axis=0
            )
            term = jnp.dot(mixers, tokens, preferred_element_type=F32)
            total = term if total is None else total + term
        for k in range(2):
            out_ref[pair + k] = total[:, k * LANES : (k + 1) * LANES].astype(BF16)


def filter_kernel(both_ref, filter_ref, skip_ref):
    for row in range(0, filter_ref.shape[0], LANES):
        rows = pl.ds(row, LANES)
        total = both_ref[0, rows] + both_ref[1, rows]
        filter_ref[rows, :] = total
        skip_ref[:, rows] = total.T[:1]


def call(kernel, name, shapes, scratch, flops, moved, vmem=32, **specs):
    return pl.pallas_call(
        kernel,
        out_shape=shapes,
        scratch_shapes=scratch,
        name=name,
        compiler_params=pltpu.CompilerParams(vmem_limit_bytes=vmem * 1024 * 1024),
        cost_estimate=pl.CostEstimate(flops=flops, bytes_accessed=moved, transcendentals=0),
        **specs,
    )


def body(grad_out, query_gate, key_gate, value_input, filter_taps, skip_gain, out_weight):
    rows, width = query_gate.shape
    norm_factor = 1.0 / math.sqrt(rows * lax.axis_size("seq"))
    gain = skip_gain.reshape(1, width)
    block_f32 = jax.ShapeDtypeStruct((rows, width), F32)
    block_bf16 = jax.ShapeDtypeStruct((rows, width), BF16)
    padded = pltpu.VMEM((2 * rows, width), F32)
    held_f32, held_bf16 = pltpu.VMEM((rows, width), F32), pltpu.VMEM((rows, width), BF16)
    held_rows = pltpu.VMEM((TAPS, LANES), F32)
    in_vmem = pl.BlockSpec(memory_space=pltpu.VMEM)
    in_hbm = pl.BlockSpec(memory_space=pltpu.HBM)
    stay = lambda value: pltpu.with_memory_space_constraint(value, pltpu.HBM)
    query, key, value = stay(query_gate), stay(key_gate), stay(value_input)
    weight = stay(out_weight)
    halves = width // LANES
    held_mixers = pltpu.VMEM((halves, LANES, rows), BF16)
    size = rows * width

    mixed_in = key_gate.astype(F32) * value_input.astype(F32)
    previous = passed_along(mixed_in, "seq", 1)
    over_zh = lax.all_gather(grad_out, "chan", axis=0, axis_index_groups=ZH_GROUPS)
    gathered = spread(over_zh, "chan", Y_GROUPS, YS)
    gathered = gathered.reshape(YS, ZH, rows, width)
    targets, blocks = ZH * CORES, YS + halves
    packed_out = pltpu.HBM((targets, blocks, rows, LANES), BF16)
    summed, packed = call(
        causal_kernel,
        "causal",
        (pltpu.HBM((rows, width), F32), packed_out),
        [
            padded,
            held_rows,
            held_bf16,
            held_f32,
            held_mixers,
            pltpu.SemaphoreType.DMA((1 + halves + targets,)),
        ],
        2 * size * TAPS,
        20 * size,
        in_specs=[in_vmem, in_vmem, in_vmem, in_vmem, in_hbm],
        out_specs=[in_hbm, in_hbm],
    )(previous, mixed_in, filter_taps, gain, query)
    packed = call(
        pack_kernel,
        "pack",
        packed_out,
        [pltpu.SemaphoreType.DMA((targets,))],
        0,
        64 * size,
        in_specs=[in_vmem, in_hbm],
        out_specs=in_hbm,
        input_output_aliases={1: 0},
    )(gathered, stay(packed))
    pieces = exchange(packed, "seq", XC_GROUPS)

    grad_query, grad_sum, filter_term = call(
        lambda *refs: main_kernel(norm_factor, *refs),
        "main",
        (block_bf16, block_f32, jax.ShapeDtypeStruct((width, TAPS), F32)),
        [
            pltpu.VMEM((ZH, width, YS * width), BF16),
            held_bf16,
            held_f32,
            padded,
            held_rows,
            pltpu.SemaphoreType.DMA((ZH,)),
            pltpu.SemaphoreType.DMA((2,)),
        ],
        2 * size * (4096 + TAPS),
        4 * 1024 * 1024,
        in_specs=[in_vmem, in_hbm, in_hbm, in_hbm, in_vmem, in_vmem],
    )(gathered, weight, query, stay(summed), previous, mixed_in)
    incoming = passed_along(grad_sum, "seq", -1)
    filter_term = jnp.sum(collect(filter_term, CORE_GROUPS), axis=0)
    filter_term = (filter_term + swapped(filter_term, 0, 1)).astype(BF16)
    from_z = swapped(filter_term, 0, 2)
    grad_key, grad_value = call(
        ahead_kernel,
        "ahead",
        (block_bf16, block_bf16),
        [
            padded,
            held_rows,
            held_bf16,
            held_bf16,
            pltpu.SemaphoreType.DMA((2,)),
        ],
        2 * size * TAPS,
        20 * size,
        in_specs=[in_vmem, in_vmem, in_vmem, in_vmem, in_hbm, in_hbm],
    )(grad_sum, incoming, filter_taps, gain, key, value)
    pieces, grad_key, grad_value = lax.optimization_barrier((pieces, grad_key, grad_value))
    partial = call(
        weight_kernel,
        "weight",
        pltpu.VMEM((ZL, width, LANES), BF16),
        [],
        2 * XS * CORES * rows * width * ZL * LANES,
        2 * 1024 * 1024,
    )(pieces)
    partial, filter_term = lax.optimization_barrier((partial, filter_term))
    filter_term = filter_term.astype(F32) + from_z.astype(F32)
    partial, filter_term = lax.optimization_barrier((partial, filter_term))
    from_x = swapped(filter_term, 1, 0)
    terms = exchange(partial, "seq", ZL_GROUPS)
    grad_filter, grad_skip = call(
        filter_kernel,
        "filter",
        (jax.ShapeDtypeStruct((width, TAPS), F32), jax.ShapeDtypeStruct((1, width), F32)),
        [],
        1 << 36,
        1 << 28,
    )(collect(filter_term + from_x, X_PAIRS))
    terms, grad_filter, grad_skip = lax.optimization_barrier((terms, grad_filter, grad_skip))
    grad_skip = grad_skip.reshape(width)
    grad_weight = jnp.sum(terms.astype(F32), axis=0) * norm_factor
    return (grad_query, grad_key, grad_value, grad_filter, grad_skip, grad_weight)


def solution(mesh):
    return jax.shard_map(
        body,
        mesh=mesh,
        in_specs=(
            P("seq", "chan"),
            P("seq", "chan"),
            P("seq", "chan"),
            P("seq", "chan"),
            P("chan", None),
            P("chan"),
            P("chan", None),
        ),
        out_specs=(
            P("seq", "chan"),
            P("seq", "chan"),
            P("seq", "chan"),
            P("chan", None),
            P("chan"),
            P("chan", "seq"),
        ),
        check_vma=False,
    )
```

```python
import math

import jax
import jax.numpy as jnp
from jax import lax
from jax.experimental import pallas as pl
from jax.experimental.pallas import tpu as pltpu
from jax.sharding import PartitionSpec as P

TAPS = 128
LANES = 128
SUB = 8
XS, ZL, CORES = 4, 4, 2
ZH, YS = 4, 4
F32 = jnp.float32
BF16 = jnp.bfloat16


def seq_index(x, zl, core):
    return (x * ZL + zl) * CORES + core


def chan_index(zh, y):
    return zh * YS + y


ZH_GROUPS = [[chan_index(zh, y) for zh in range(ZH)] for y in range(YS)]
Y_GROUPS = [[chan_index(zh, y) for y in range(YS)] for zh in range(ZH)]
XC_GROUPS = [
    [seq_index(x, zl, core) for x in range(XS) for core in range(CORES)] for zl in range(ZL)
]
ZL_GROUPS = [
    [seq_index(x, zl, core) for zl in range(ZL)] for x in range(XS) for core in range(CORES)
]
X_PAIRS = [
    [seq_index(x + half, zl, core) for half in (0, XS // 2)]
    for x in range(XS // 2)
    for zl in range(ZL)
    for core in range(CORES)
]
CORE_GROUPS = [
    [seq_index(x, zl, core) for core in range(CORES)] for x in range(XS) for zl in range(ZL)
]


def exchange(value, axis, groups):
    return lax.all_to_all(value, axis, 0, 0, tiled=True, axis_index_groups=groups)


def spread(value, axis, groups, size):
    return exchange(jnp.broadcast_to(value[None], (size, *value.shape)), axis, groups)


def collect(value, groups):
    return lax.all_gather(value, "seq", axis=0, axis_index_groups=groups)


def swapped(value, flip_x, flip_z):
    pairs = [
        (seq_index(x, zl, core), seq_index(x ^ flip_x, zl ^ flip_z, core))
        for x in range(XS)
        for zl in range(ZL)
        for core in range(CORES)
    ]
    return lax.ppermute(value, "seq", pairs)


def passed_along(value, axis, by):
    size = lax.axis_size(axis)
    pairs = [(i, i + by) for i in range(size) if 0 <= i + by < size]
    return lax.ppermute(value, axis, pairs)


def fetch(sources, held, sem, first=0):
    copies = [
        pltpu.make_async_copy(source, target, sem.at[first + at])
        for at, (source, target) in enumerate(zip(sources, held))
    ]
    for copy in copies:
        copy.start()
    return copies


def finish(copies):
    for copy in copies:
        copy.wait()


def weighted(shifted, tap_rows, starts, rows):
    part = None
    for tap, start in starts:
        term = tap_rows[tap : tap + 1, :] * shifted[start : start + rows]
        part = term if part is None else part + term
    return part


def causal_kernel(
    prev_ref,
    mixed_ref,
    taps_ref,
    gain_ref,
    query_ref,
    summed_ref,
    packed_ref,
    pad,
    tap_rows,
    query,
    summed,
    mixers,
    sem,
):
    copies = fetch((query_ref,), (query,), sem)
    stores = []
    rows, width = mixed_ref.shape
    pad[:rows] = prev_ref[...]
    pad[rows:] = mixed_ref[...]
    for lane in range(0, width, LANES):
        cols = pl.ds(lane, LANES)
        tap_rows[...] = taps_ref[cols, :].T
        total = gain_ref[:, cols] * mixed_ref[:, cols]
        for r in range(SUB):
            shifted = pad[pl.ds(SUB - r, 2 * rows - SUB), cols]
            starts = [(SUB * q + r, rows - SUB - SUB * q) for q in range(TAPS // SUB)]
            total = total + weighted(shifted, tap_rows, starts, rows)
        summed[:, cols] = total
        stores += fetch((summed.at[:, cols],), (summed_ref.at[:, cols],), sem, 1 + lane // LANES)
        if lane == 0:
            finish(copies)
        mixers[lane // LANES] = (query[:, cols].astype(F32) * total).T.astype(BF16)
    targets, halves = packed_ref.shape[0], mixers.shape[0]
    places = [packed_ref.at[target, pl.ds(YS, halves)] for target in range(targets)]
    finish(stores + fetch([mixers] * targets, places, sem, 1 + halves))


def pack_kernel(gathered_ref, begun_ref, packed_ref, sem):
    del begun_ref
    targets = [(zh, core) for zh in range(ZH) for core in range(CORES)]
    sources = [gathered_ref.at[:, zh, :, pl.ds(core * LANES, LANES)] for zh, core in targets]
    places = [packed_ref.at[zh * CORES + core, pl.ds(0, YS)] for zh, core in targets]
    finish(fetch(sources, places, sem))


def main_kernel(
    norm_factor,
    gathered_ref,
    weight_ref,
    query_ref,
    summed_ref,
    prev_ref,
    mixed_ref,
    grad_query_ref,
    grad_sum_ref,
    filter_ref,
    held,
    query,
    summed,
    pad,
    tap_rows,
    weight_sem,
    sem,
):
    rows, width = mixed_ref.shape
    loads = []
    for zh in range(ZH):
        cols = pl.ds(zh * YS * width, YS * width)
        loads.append(pltpu.make_async_copy(weight_ref.at[:, cols], held.at[zh], weight_sem.at[zh]))
        loads[-1].start()
    blocks = fetch((query_ref, summed_ref), (query, summed), sem)
    pad[:rows] = prev_ref[...]
    pad[rows:] = mixed_ref[...]

    total = None
    finish(loads)
    for zh in range(ZH):
        for y in range(YS):
            term = lax.dot_general(
                gathered_ref[y, zh],
                held[zh, :, pl.ds(y * width, width)],
                (((1,), (1,)), ((), ())),
                preferred_element_type=F32,
            )
            total = term if total is None else total + term
    finish(blocks)
    grad_query_ref[...] = (total * summed[...]).astype(BF16)
    grad_sum_ref[...] = total * query[...].astype(F32)

    for lane in range(0, width, LANES):
        cols = pl.ds(lane, LANES)
        grad_sum = grad_sum_ref[:, cols]
        for r in range(SUB):
            shifted = pad[pl.ds(SUB - r, 2 * rows - SUB), cols]
            for q in range(TAPS // SUB):
                start = rows - SUB - SUB * q
                j = SUB * q + r
                tap_rows[j : j + 1, :] = jnp.sum(
                    grad_sum * shifted[start : start + rows], axis=0, keepdims=True
                )
        filter_ref[cols, :] = tap_rows[...].T * norm_factor


def ahead_kernel(
    grad_sum_ref,
    incoming_ref,
    taps_ref,
    gain_ref,
    key_ref,
    value_ref,
    grad_key_ref,
    grad_value_ref,
    pad,
    tap_rows,
    key,
    value,
    sem,
):
    copies = fetch((key_ref, value_ref), (key, value), sem)
    rows, width = grad_sum_ref.shape
    pad[:rows] = grad_sum_ref[...]
    pad[rows:] = incoming_ref[...]
    for lane in range(0, width, LANES):
        cols = pl.ds(lane, LANES)
        tap_rows[...] = taps_ref[cols, :].T
        total = gain_ref[:, cols] * grad_sum_ref[:, cols]
        for r in range(SUB):
            shifted = pad[pl.ds(r, 2 * rows - SUB), cols]
            starts = [(SUB * q + r, SUB * q) for q in range(TAPS // SUB)]
            total = total + weighted(shifted, tap_rows, starts, rows)
        if lane == 0:
            finish(copies)
        grad_key_ref[:, cols] = (total * value[:, cols].astype(F32)).astype(BF16)
        grad_value_ref[:, cols] = (total * key[:, cols].astype(F32)).astype(BF16)


def weight_kernel(pieces_ref, out_ref):
    def side_by_side(blocks):
        return jnp.concatenate(blocks, axis=1)

    halves = pieces_ref.shape[1] - ZL
    for pair in range(0, ZL, 2):
        total = None
        for x in range(XS):
            sources = range(CORES * x, CORES * (x + 1))
            mixers = jnp.concatenate(
                [side_by_side([pieces_ref[at, ZL + half] for at in sources]) for half in range(halves)],
                axis=0,
            )
            tokens = jnp.concatenate(
                [side_by_side([pieces_ref[at, pair + k] for k in range(2)]) for at in sources], axis=0
            )
            term = jnp.dot(mixers, tokens, preferred_element_type=F32)
            total = term if total is None else total + term
        for k in range(2):
            out_ref[pair + k] = total[:, k * LANES : (k + 1) * LANES].astype(BF16)


def filter_kernel(both_ref, filter_ref, skip_ref):
    for row in range(0, filter_ref.shape[0], LANES):
        rows = pl.ds(row, LANES)
        total = both_ref[0, rows] + both_ref[1, rows]
        filter_ref[rows, :] = total
        skip_ref[:, rows] = total.T[:1]


def call(kernel, name, shapes, scratch, flops, moved, vmem=32, **specs):
    return pl.pallas_call(
        kernel,
        out_shape=shapes,
        scratch_shapes=scratch,
        name=name,
        compiler_params=pltpu.CompilerParams(vmem_limit_bytes=vmem * 1024 * 1024),
        cost_estimate=pl.CostEstimate(flops=flops, bytes_accessed=moved, transcendentals=0),
        **specs,
    )


def body(grad_out, query_gate, key_gate, value_input, filter_taps, skip_gain, out_weight):
    rows, width = query_gate.shape
    norm_factor = 1.0 / math.sqrt(rows * lax.axis_size("seq"))
    gain = skip_gain.reshape(1, width)
    block_f32 = jax.ShapeDtypeStruct((rows, width), F32)
    block_bf16 = jax.ShapeDtypeStruct((rows, width), BF16)
    padded = pltpu.VMEM((2 * rows, width), F32)
    held_f32, held_bf16 = pltpu.VMEM((rows, width), F32), pltpu.VMEM((rows, width), BF16)
    held_rows = pltpu.VMEM((TAPS, LANES), F32)
    in_vmem = pl.BlockSpec(memory_space=pltpu.VMEM)
    in_hbm = pl.BlockSpec(memory_space=pltpu.HBM)
    stay = lambda value: pltpu.with_memory_space_constraint(value, pltpu.HBM)
    query, key, value = stay(query_gate), stay(key_gate), stay(value_input)
    weight = stay(out_weight)
    halves = width // LANES
    held_mixers = pltpu.VMEM((halves, LANES, rows), BF16)
    size = rows * width

    mixed_in = key_gate.astype(F32) * value_input.astype(F32)
    previous = passed_along(mixed_in, "seq", 1)
    over_zh = lax.all_gather(grad_out, "chan", axis=0, axis_index_groups=ZH_GROUPS)
    gathered = spread(over_zh, "chan", Y_GROUPS, YS)
    gathered = gathered.reshape(YS, ZH, rows, width)
    targets, blocks = ZH * CORES, YS + halves
    packed_out = pltpu.HBM((targets, blocks, rows, LANES), BF16)
    summed, packed = call(
        causal_kernel,
        "causal",
        (pltpu.HBM((rows, width), F32), packed_out),
        [
            padded,
            held_rows,
            held_bf16,
            held_f32,
            held_mixers,
            pltpu.SemaphoreType.DMA((1 + halves + targets,)),
        ],
        2 * size * TAPS,
        20 * size,
        in_specs=[in_vmem, in_vmem, in_vmem, in_vmem, in_hbm],
        out_specs=[in_hbm, in_hbm],
    )(previous, mixed_in, filter_taps, gain, query)
    packed = call(
        pack_kernel,
        "pack",
        packed_out,
        [pltpu.SemaphoreType.DMA((targets,))],
        0,
        64 * size,
        in_specs=[in_vmem, in_hbm],
        out_specs=in_hbm,
        input_output_aliases={1: 0},
    )(gathered, stay(packed))
    pieces = exchange(packed, "seq", XC_GROUPS)

    grad_query, grad_sum, filter_term = call(
        lambda *refs: main_kernel(norm_factor, *refs),
        "main",
        (block_bf16, block_f32, jax.ShapeDtypeStruct((width, TAPS), F32)),
        [
            pltpu.VMEM((ZH, width, YS * width), BF16),
            held_bf16,
            held_f32,
            padded,
            held_rows,
            pltpu.SemaphoreType.DMA((ZH,)),
            pltpu.SemaphoreType.DMA((2,)),
        ],
        2 * size * (4096 + TAPS),
        4 * 1024 * 1024,
        in_specs=[in_vmem, in_hbm, in_hbm, in_hbm, in_vmem, in_vmem],
    )(gathered, weight, query, stay(summed), previous, mixed_in)
    incoming = passed_along(grad_sum, "seq", -1)
    filter_term = jnp.sum(collect(filter_term, CORE_GROUPS), axis=0)
    filter_term = (filter_term + swapped(filter_term, 0, 1)).astype(BF16)
    from_z = swapped(filter_term, 0, 2)
    grad_key, grad_value = call(
        ahead_kernel,
        "ahead",
        (block_bf16, block_bf16),
        [
            padded,
            held_rows,
            held_bf16,
            held_bf16,
            pltpu.SemaphoreType.DMA((2,)),
        ],
        2 * size * TAPS,
        20 * size,
        in_specs=[in_vmem, in_vmem, in_vmem, in_vmem, in_hbm, in_hbm],
    )(grad_sum, incoming, filter_taps, gain, key, value)
    pieces, grad_key, grad_value = lax.optimization_barrier((pieces, grad_key, grad_value))
    partial = call(
        weight_kernel,
        "weight",
        pltpu.VMEM((ZL, width, LANES), BF16),
        [],
        2 * XS * CORES * rows * width * ZL * LANES,
        2 * 1024 * 1024,
    )(pieces)
    partial, filter_term = lax.optimization_barrier((partial, filter_term))
    filter_term = filter_term.astype(F32) + from_z.astype(F32)
    partial, filter_term = lax.optimization_barrier((partial, filter_term))
    from_x = swapped(filter_term, 1, 0)
    terms = exchange(partial, "seq", ZL_GROUPS)
    grad_filter, grad_skip = call(
        filter_kernel,
        "filter",
        (jax.ShapeDtypeStruct((width, TAPS), F32), jax.ShapeDtypeStruct((1, width), F32)),
        [],
        1 << 36,
        1 << 28,
    )(collect(filter_term + from_x, X_PAIRS))
    terms, grad_filter, grad_skip = lax.optimization_barrier((terms, grad_filter, grad_skip))
    grad_skip = grad_skip.reshape(width)
    grad_weight = jnp.sum(terms.astype(F32), axis=0) * norm_factor
    return (grad_query, grad_key, grad_value, grad_filter, grad_skip, grad_weight)


def solution(mesh):
    return jax.shard_map(
        body,
        mesh=mesh,
        in_specs=(
            P("seq", "chan"),
            P("seq", "chan"),
            P("seq", "chan"),
            P("seq", "chan"),
            P("chan", None),
            P("chan"),
            P("chan", None),
        ),
        out_specs=(
            P("seq", "chan"),
            P("seq", "chan"),
            P("seq", "chan"),
            P("chan", None),
            P("chan"),
            P("chan", "seq"),
        ),
        check_vma=False,
    )
```
